512 devices in a mesh: lat: 32 (over z_lo, y), lon: 16 (over x, z_hi, core).
Axes of the slice: x: 4, y: 8, z: 8 (z_hi: 2, z_lo: 4; z = z_hi * 4 + z_lo), core: 2. Of those that a mesh axis runs over, the one named last changes fastest.
Arguments:
- activations: bfloat16 [128, 512, 256], P('lat', 'lon'), may hold values from -23 to 23
- basis_weights: bfloat16 [9, 128, 7, 7], replicated, may hold values from -0.875 to 0.875
- extents: int32 [2, 128, 7], replicated, may hold values from 0 to 3
- mix_weight: bfloat16 [9, 16, 16, 16], replicated, may hold values from -0.5 to 0.5
- spec_filter: float32 [2, 256, 128], P(None, 'lon'), may hold values from -6 to 6
- w_in: bfloat16 [256, 512], replicated, may hold values from -0.375 to 0.375
- w_out: bfloat16 [512, 256], replicated, may hold values from -0.25 to 0.25
- cotangent: bfloat16 [128, 512, 256], P('lat', 'lon'), may hold values from -6 to 6
Outputs:
- block_output: bfloat16 [128, 512, 256], P('lat', 'lon')
- grad_x: bfloat16 [128, 512, 256], P('lat', 'lon')
- grad_filter: float32 [2, 256, 128], P(None, 'lon')
The draws below stay inside these ranges and needn't reach their ends.
All inputs are finite; a program needn't handle non-finite values.
Results may differ from the reference program's by a relative error of at most 0.02.
Values may be sent and summed in bfloat16 or wider, within the bound.
A program may use at most 128 MiB of HBM per device.

```python
import math
import jax
import jax.numpy as jnp
from jax import lax

C = 256
HID = 512
BASIS = 9
GROUP = 16
REACH = 3
NLAT = 128
NLON = 512


def draw_activations(key, part):
    key = jax.random.fold_in(key, 17)
    base_key, lane_key, cell_key = jax.random.split(key, 3)
    lane_scale = jnp.exp(jax.random.uniform(lane_key, (C,), jnp.float32, math.log(0.3), math.log(3.0)))
    cell_scale = jnp.exp(jax.random.uniform(cell_key, (NLAT, NLON, 1), jnp.float32, math.log(0.3), math.log(3.0)))
    base = jnp.clip(jax.random.normal(base_key, (NLAT, NLON, C), jnp.float32), -5.0, 5.0)
    return (0.5 * base * lane_scale * cell_scale).astype(jnp.bfloat16)


def with_ends(drawn, stream_key, low, largest):
    longest = drawn.shape.index(max(drawn.shape))
    spots = []
    for shift in (0, 1):
        where = [jax.random.randint(jax.random.fold_in(stream_key, axis), (), 0, length) for axis, length in enumerate(drawn.shape)]
        where[longest] = (where[longest] + shift) % drawn.shape[longest]
        spots.append(tuple(where))
    return drawn.at[spots[0]].set(low).at[spots[1]].set(largest)


def level_of(rng, dims, cuts, smallest, largest):
    loudness = 1.0
    for axis_at, parts in cuts:
        steps = jax.random.uniform(jax.random.fold_in(jax.random.fold_in(rng, 6), axis_at), (parts,), jnp.float32, smallest / len(cuts), largest / len(cuts))
        loudness = loudness * jnp.repeat(jnp.exp(steps), dims[axis_at] // parts).reshape((-1,) + (1,) * (len(dims) - 1 - axis_at))
    return loudness


def noise(key, shape, scale, most, cuts=(), kind=jnp.bfloat16):
    array = jax.random.normal(key, shape, jnp.float32) * scale
    if len(cuts) > 0:
        array = level_of(key, shape, cuts, -0.22, 0.18) * array
    return jnp.clip(array, min=-most, max=most).astype(kind)


def setup_inputs(seed: int = 0) -> dict:
    arg_keys = jax.random.split(jax.random.key(seed), 9)
    activations = draw_activations(jax.random.fold_in(arg_keys[8], 71), 0)
    basis_weights = noise(arg_keys[1], (BASIS, NLAT, 2 * REACH + 1, 2 * REACH + 1), ((2 * REACH + 1) * (2 * REACH + 1)) ** -0.5, 0.875)
    extents = with_ends(jax.random.randint(arg_keys[2], (2, NLAT, 2 * REACH + 1), 0, REACH + 1), jax.random.fold_in(arg_keys[2], 1), 0, REACH).astype(jnp.int32)
    mix_weight = noise(arg_keys[3], (BASIS, C // GROUP, GROUP, GROUP), (BASIS * GROUP) ** -0.5, 0.5)
    spec_filter = noise(arg_keys[4], (2, C, NLAT), 1.0, 6.0, ((1, 16),), jnp.float32)
    w_in = noise(arg_keys[5], (C, HID), C ** -0.5, 0.375)
    w_out = noise(arg_keys[6], (HID, C), HID ** -0.5, 0.25)
    cotangent = noise(arg_keys[7], (NLAT, NLON, C), 1.0, 6.0, ((0, 32), (1, 16)))
    return dict(activations=activations, basis_weights=basis_weights, extents=extents, mix_weight=mix_weight, spec_filter=spec_filter, w_in=w_in, w_out=w_out, cotangent=cotangent)


HIGHEST = lax.Precision.HIGHEST
EPSILON = 1e-05

def layer_norm(values):
    centred = values - lax.optimization_barrier(jnp.mean(values, axis=-1, keepdims=True))
    inverse = lax.rsqrt(lax.optimization_barrier(jnp.mean(centred * centred, axis=-1, keepdims=True)) + EPSILON)
    return (centred * inverse, inverse)

def norm_back(normed, inverse, upstream):
    return inverse * (upstream - lax.optimization_barrier(jnp.mean(upstream, axis=-1, keepdims=True)) - normed * lax.optimization_barrier(jnp.mean(upstream * normed, axis=-1, keepdims=True)))

def gelu_slope(values):
    return 0.5 * (1.0 + jax.scipy.special.erf(values * (1.0 / math.sqrt(2.0)))) + values * jnp.exp(-0.5 * values * values) * (1.0 / math.sqrt(2.0 * math.pi))

def quad_weights(lat_total):
    theta = math.pi * (jnp.arange(lat_total, dtype=jnp.float32) + 0.5) / lat_total
    return math.pi / lat_total * jnp.sin(theta)

def legendre_table(orders, lat_total, degree_total, order_total):
    theta = math.pi * (jnp.arange(lat_total, dtype=jnp.float32) + 0.5) / lat_total
    cosine = jnp.cos(theta)
    log_sine = jnp.log(jnp.sin(theta))
    counter = jnp.arange(1, order_total, dtype=jnp.int32).astype(jnp.float32)
    growth = jnp.concatenate([jnp.zeros((1,), jnp.float32), jnp.cumsum(0.5 * jnp.log((2.0 * counter + 1.0) / (2.0 * counter)))])
    order_float = orders.astype(jnp.float32)
    diagonal = jnp.exp(-0.5 * math.log(4.0 * math.pi) + jnp.take(growth, orders)[:, None] + order_float[:, None] * log_sine[None, :])

    def advance(carry, degree):
        latest, earlier = carry
        degree_float = degree.astype(jnp.float32)
        upper = jnp.sqrt(jnp.maximum(4.0 * degree_float * degree_float - 1.0, 1.0) / jnp.maximum(degree_float * degree_float - order_float * order_float, 1.0))
        below = degree_float - 1.0
        lower_coef = jnp.sqrt(jnp.maximum(below * below - order_float * order_float, 0.0) / jnp.maximum(4.0 * below * below - 1.0, 1.0))
        recurred = upper[:, None] * (cosine[None, :] * latest - lower_coef[:, None] * earlier)
        value = jnp.where(degree < orders[:, None], jnp.zeros_like(recurred), jnp.where(degree == orders[:, None], diagonal, recurred))
        return ((value, latest), value)
    zeros = jnp.zeros((orders.shape[0], lat_total), jnp.float32)
    final, table = lax.scan(advance, (zeros, zeros), jnp.arange(degree_total, dtype=jnp.int32), unroll=8)
    return table

def keep_taps(weights, extents):
    tap_total = weights.shape[-1]
    shift = jnp.arange(tap_total, dtype=jnp.int32) - (tap_total - 1) // 2
    inside = (shift >= -extents[0][..., None]) & (shift <= extents[1][..., None])
    return jnp.where(inside, weights, jnp.zeros_like(weights))

def round_trip(values):
    return lax.optimization_barrier(values.astype(jnp.bfloat16)).astype(jnp.float32)

def lon_synthesis(real_part, imag_part, lon_total):
    values = lax.complex(real_part, imag_part)
    values = jnp.pad(values, ((0, 0), (0, lon_total // 2 + 1 - real_part.shape[1]), (0, 0)))
    return jnp.fft.irfft(values, n=lon_total, axis=1)

def reference(activations, basis_weights, extents, mix_weight, spec_filter, w_in, w_out, cotangent):
    tap_count = 2 * REACH + 1
    group_count = C // GROUP
    source = activations.astype(jnp.float32)
    normed_in, inverse_in = layer_norm(source)
    kept = keep_taps(basis_weights, extents).astype(jnp.float32)
    wrapped = (jnp.arange(tap_count, dtype=jnp.int32) - REACH) % NLON
    kernel = jnp.zeros((BASIS, NLAT, tap_count, NLON), jnp.float32).at[:, :, :, wrapped].set(kept)
    kernel_freq = jnp.fft.rfft(kernel, axis=-1)
    field_freq = jnp.fft.rfft(round_trip(normed_in), axis=1)
    padded = jnp.pad(field_freq, ((REACH, REACH), (0, 0), (0, 0)))

    def forward_basis(total, inputs):
        basis_freq, weight = inputs
        summed = jnp.zeros_like(field_freq)
        for offset in range(tap_count):
            summed = summed + jnp.conj(basis_freq[:, offset, :])[:, :, None] * padded[offset:offset + NLAT]
        filtered = round_trip(jnp.fft.irfft(summed, n=NLON, axis=1))
        total = total + jnp.einsum('lngi,gio->lngo', filtered.reshape(NLAT, NLON, group_count, GROUP), weight.astype(jnp.float32), precision=HIGHEST)
        return (total, None)
    mix_total, unused = lax.scan(forward_basis, jnp.zeros((NLAT, NLON, group_count, GROUP), jnp.float32), (kernel_freq, mix_weight))
    mixed_in = round_trip(mix_total.reshape(NLAT, NLON, C))
    orders = jnp.arange(NLAT, dtype=jnp.int32)
    legendre = legendre_table(orders, NLAT, NLAT, NLAT)
    quadrature = quad_weights(NLAT)
    order_weight = jnp.where(orders == 0, 1.0, 2.0).astype(jnp.float32)
    spectrum = jnp.fft.rfft(mixed_in, axis=1)[:, :NLAT, :] * (2.0 * math.pi / NLON)
    four_real = jnp.real(spectrum) * quadrature[:, None, None]
    four_imag = jnp.imag(spectrum) * quadrature[:, None, None]
    coef_real = jnp.einsum('lmt,tmc->mlc', legendre, four_real, precision=HIGHEST)
    coef_imag = jnp.einsum('lmt,tmc->mlc', legendre, four_imag, precision=HIGHEST)
    filter_real = spec_filter[0].T[None]
    filter_imag = spec_filter[1].T[None]
    prod_real = coef_real * filter_real - coef_imag * filter_imag
    prod_imag = coef_real * filter_imag + coef_imag * filter_real
    synth_real = jnp.einsum('lmt,mlc->tmc', legendre, prod_real, precision=HIGHEST)
    synth_imag = jnp.einsum('lmt,mlc->tmc', legendre, prod_imag, precision=HIGHEST)
    spectral = NLON * lon_synthesis(synth_real, synth_imag, NLON)
    carried = source + spectral
    normed_mid, inverse_mid = layer_norm(carried)
    middle = normed_mid.astype(jnp.bfloat16).reshape(-1, C)
    preact = jnp.dot(middle, w_in, preferred_element_type=jnp.float32)
    hidden = jax.nn.gelu(preact, approximate=False).astype(jnp.bfloat16)
    block_output = (carried + jnp.dot(hidden, w_out, preferred_element_type=jnp.float32).reshape(NLAT, NLON, C)).astype(jnp.bfloat16)
    flat_cot = cotangent.reshape(-1, C)
    d_hidden = jnp.dot(flat_cot, w_out.T, preferred_element_type=jnp.float32)
    d_preact = (d_hidden * gelu_slope(preact)).astype(jnp.bfloat16)
    d_normed = jnp.dot(d_preact, w_in.T, preferred_element_type=jnp.float32).reshape(NLAT, NLON, C)
    d_carried = cotangent.astype(jnp.float32) + norm_back(normed_mid, inverse_mid, d_normed)
    d_freq = jnp.fft.rfft(round_trip(d_carried), axis=1)[:, :NLAT, :] * order_weight[None, :, None]
    dp_real = jnp.einsum('lmt,tmc->mlc', legendre, jnp.real(d_freq), precision=HIGHEST)
    dp_imag = jnp.einsum('lmt,tmc->mlc', legendre, jnp.imag(d_freq), precision=HIGHEST)
    grad_real = lax.optimization_barrier(jnp.sum(dp_real * coef_real + dp_imag * coef_imag, axis=0)).T
    grad_imag = lax.optimization_barrier(jnp.sum(dp_imag * coef_real - dp_real * coef_imag, axis=0)).T
    dc_real = dp_real * filter_real + dp_imag * filter_imag
    dc_imag = dp_imag * filter_real - dp_real * filter_imag
    df_real = quadrature[:, None, None] * jnp.einsum('lmt,mlc->tmc', legendre, dc_real, precision=HIGHEST) / order_weight[None, :, None]
    df_imag = quadrature[:, None, None] * jnp.einsum('lmt,mlc->tmc', legendre, dc_imag, precision=HIGHEST) / order_weight[None, :, None]
    d_mixed = round_trip(2.0 * math.pi * lon_synthesis(df_real, df_imag, NLON))
    grouped = d_mixed.reshape(NLAT, NLON, group_count, GROUP)

    def backward_basis(total, inputs):
        basis_freq, weight = inputs
        d_filtered = round_trip(jnp.einsum('lngo,gio->lngi', grouped, weight.astype(jnp.float32), precision=HIGHEST)).reshape(NLAT, NLON, C)
        grad_freq = jnp.fft.rfft(d_filtered, axis=1)
        for offset in range(tap_count):
            total = total.at[offset:offset + NLAT].add(basis_freq[:, offset, :][:, :, None] * grad_freq)
        return (total, None)
    summed_freq, unused = lax.scan(backward_basis, jnp.zeros(padded.shape, padded.dtype), (kernel_freq, mix_weight))
    d_normed_in = jnp.fft.irfft(summed_freq[REACH:REACH + NLAT], n=NLON, axis=1)
    grad_x = (d_carried + norm_back(normed_in, inverse_in, d_normed_in)).astype(jnp.bfloat16)
    grad_filter = jnp.stack([grad_real, grad_imag])
    return (block_output, grad_x, grad_filter)
```

```python
import math

import jax
import jax.numpy as jnp
import numpy as np
from jax import lax
from jax.experimental import pallas as pl
from jax.experimental.pallas import tpu as pltpu
from jax.sharding import PartitionSpec as P

EPSILON = 1e-05
MESH = pl.DeviceIdType.MESH
F32 = jnp.float32
BF16 = jnp.bfloat16

NLAT = 128
NLON = 512
CHANS = 256
HIDDEN = 512
BASIS = 9
GROUP = 16
TAPS = 7
REACH = 3
LATS = 32
ROWS = 4
COLS = 32
ORDERS = 4
PARTS = 8
NEAR = 8
FAR = 64


def legendre_values():
    theta = math.pi * (np.arange(NLAT) + 0.5) / NLAT
    cosine, sine = (np.cos(theta), np.sin(theta))
    table = np.zeros((NLAT, NLAT, NLAT))
    for order in range(NLAT):
        steps = np.arange(1, order + 1)
        growth = np.sum(0.5 * np.log((2.0 * steps + 1.0) / (2.0 * steps)))
        earlier = np.zeros(NLAT)
        latest = np.exp(-0.5 * math.log(4.0 * math.pi) + growth + order * np.log(sine))
        table[order, order] = latest
        for degree in range(order + 1, NLAT):
            upper = math.sqrt((4.0 * degree**2 - 1.0) / (degree**2 - order**2))
            below = degree - 1.0
            lower = math.sqrt((below**2 - order**2) / (4.0 * below**2 - 1.0))
            earlier, latest = (latest, upper * (cosine * latest - lower * earlier))
            table[order, degree] = latest
    return table.astype(np.float32).reshape(LATS, ORDERS, NLAT, NLAT)


def trig_values():
    table = np.zeros((2, ORDERS, 2, LATS, NEAR, COLS))
    order = 4 * np.arange(LATS)[None, :] + np.arange(ORDERS)[:, None]
    for half in range(2):
        for near in range(NEAR):
            lon = 32 * ((near // 2) * 4 + half * 2 + near % 2) + np.arange(COLS)
            angle = (order[:, :, None] * lon[None, None, :] % NLON) * (2.0 * math.pi / NLON)
            table[half, :, 0, :, near] = np.cos(angle)
            table[half, :, 1, :, near] = -np.sin(angle)
    return table.astype(np.float32).reshape(2, PARTS * LATS, NEAR * COLS)


def phase_values():
    order = 4 * np.arange(LATS)[:, None] + np.arange(ORDERS)[None, :]
    shift = np.arange(TAPS) - REACH
    angle = order[:, None, :] * shift[None, :, None] * (2.0 * math.pi / NLON)
    pairs = np.stack([np.cos(angle), np.sin(angle)], axis=-1).reshape(LATS, TAPS, PARTS, 1)
    return np.broadcast_to(pairs, (LATS, TAPS, PARTS, 128)).astype(np.float32).copy()


def quad_values():
    theta = math.pi * (np.arange(NLAT) + 0.5) / NLAT
    weights = (2.0 * math.pi / NLON) * (math.pi / NLAT) * np.sin(theta)
    return np.broadcast_to(weights[None], (8, NLAT)).astype(np.float32).copy()


def mm(left, right, left_dim=1, right_dim=0):
    return lax.dot_general(
        left, right, (((left_dim,), (right_dim,)), ((), ())), preferred_element_type=F32
    )


def split(values):
    high = values.astype(BF16)
    return (high, (values - high.astype(F32)).astype(BF16))


def swap_blocks(blocks, width):
    blocks = list(blocks)
    lane = lax.broadcasted_iota(jnp.int32, blocks[0].shape, 1)
    stride = 1
    while stride < len(blocks):
        keep = (lane & (stride * width)) == 0
        for at in range(len(blocks)):
            if at & stride == 0:
                low, high = (blocks[at], blocks[at | stride])
                blocks[at] = jnp.where(keep, low, pltpu.roll(high, stride * width, 1))
                blocks[at | stride] = jnp.where(keep, pltpu.roll(low, 128 - stride * width, 1), high)
        stride *= 2
    return blocks


def layer_norm(values):
    centred = values - jnp.mean(values, axis=0, keepdims=True)
    inverse = lax.rsqrt(jnp.mean(centred * centred, axis=0, keepdims=True) + EPSILON)
    return (centred * inverse, inverse)


def norm_back(normed, inverse, upstream):
    return inverse * (
        upstream
        - jnp.mean(upstream, axis=0, keepdims=True)
        - normed * jnp.mean(upstream * normed, axis=0, keepdims=True)
    )


def near_of(group):
    return ((group // 4) * 2 + group % 2, (group // 2) % 2)


def body(
    x_ref,
    cot_ref,
    basis_ref,
    ext_ref,
    filt_ref,
    quad_ref,
    mix_hbm,
    win_hbm,
    wout_hbm,
    leg_hbm,
    trig_hbm,
    phase_hbm,
    out_ref,
    gx_ref,
    gf_ref,
    send_near,
    recv_near,
    send_far,
    recv_far,
    grad_send,
    grad_recv,
    grad_row,
    grad_all,
    mix_v,
    win_v,
    wout_v,
    leg_v,
    leg_hi,
    leg_lo,
    trig_v,
    trig_hi,
    trig_lo,
    phase_v,
    taps_v,
    xt_v,
    normed_v,
    cott_v,
    dhid_v,
    wint_v,
    woutt_v,
    conv_v,
    coef_v,
    dcar_v,
    load_sem,
    send_sem,
    recv_sem,
):
    lat = lax.axis_index("lat")
    lon = lax.axis_index("lon")
    x_at, half, core = (lon // 4, lax.rem(lon // 2, 2), lax.rem(lon, 2))
    near_me = x_at * 2 + core
    far_me = half * LATS + lat
    z_me, y_me = (far_me // 8, lax.rem(far_me, 8))

    loads = []
    for index, (source, target) in enumerate(
        (
            (trig_hbm.at[half], trig_v),
            (phase_hbm.at[lat], phase_v),
            (leg_hbm.at[lat], leg_v),
            (mix_hbm.at[:, lon], mix_v),
            (win_hbm, win_v),
            (wout_hbm, wout_v),
        )
    ):
        copy = pltpu.make_async_copy(source, target, load_sem.at[index])
        copy.start()
        loads.append(copy)

    def near_peer(step):
        step = step + (step >= 4).astype(jnp.int32)
        peer = lax.rem(near_me + 4 + step, NEAR)
        return (peer, (lat, (peer // 2) * 4 + half * 2 + lax.rem(peer, 2)))

    def far_peer(step):
        step = step + (step >= 36).astype(jnp.int32)
        peer_z = lax.rem(z_me + 4 + step // 8, 8)
        peer_y = lax.rem(y_me + 4 + lax.rem(step, 8), 8)
        peer = peer_z * 8 + peer_y
        return (peer, (lax.rem(peer, LATS), x_at * 4 + (peer // LATS) * 2 + core))

    def loop(count, action):
        def run(step, carry):
            action(step)
            return carry

        lax.fori_loop(0, count, run, 0)

    barrier = pltpu.get_barrier_semaphore()

    def greet(peer_of):
        def action(step):
            peer, device = peer_of(step)
            pl.semaphore_signal(barrier, inc=1, device_id=device, device_id_type=MESH)

        return action

    loop(FAR - 1, greet(far_peer))
    loop(NEAR - 1, greet(near_peer))

    def start_near(at):
        def action(step):
            peer, device = near_peer(step)
            pltpu.make_async_remote_copy(
                src_ref=send_near.at[at, peer],
                dst_ref=recv_near.at[at, near_me],
                send_sem=send_sem.at[at],
                recv_sem=recv_sem.at[at],
                device_id=device,
                device_id_type=MESH,
            ).start()

        loop(NEAR - 1, action)
        recv_near[at, near_me] = send_near[at, near_me]

    def wait_near(at):
        block = recv_near.at[at, pl.ds(0, NEAR - 1)]
        pltpu.make_async_copy(block, block, recv_sem.at[at]).wait()

    def start_far(at, both):
        def action(step):
            peer, device = far_peer(step)
            pltpu.make_async_remote_copy(
                src_ref=send_far.at[at, lax.rem(peer, LATS) if both else peer],
                dst_ref=recv_far.at[at, far_me],
                send_sem=send_sem.at[4 + at],
                recv_sem=recv_sem.at[4 + at],
                device_id=device,
                device_id_type=MESH,
            ).start()

        loop(FAR - 1, action)
        recv_far[at, far_me] = send_far[at, lat if both else far_me]

    def wait_far(at):
        block = recv_far.at[at, pl.ds(0, FAR - 1)]
        pltpu.make_async_copy(block, block, recv_sem.at[4 + at]).wait()

    def send_field(at, field):
        for group in range(CHANS // GROUP):
            near, part = near_of(group)
            send_near[at, near, part * GROUP : (part + 1) * GROUP, :] = field[
                group * GROUP : (group + 1) * GROUP
            ].astype(BF16)
        start_near(at)

    def take_field(at):
        pieces = []
        for group in range(CHANS // GROUP):
            near, part = near_of(group)
            pieces.append(recv_near[at, near, part * GROUP : (part + 1) * GROUP, :].astype(F32))
        return jnp.concatenate(pieces, axis=0)

    def to_spectrum(near_at, far_at):
        rows = [recv_near[near_at, near].astype(F32) for near in range(NEAR)]
        first = swap_blocks(rows[:4], COLS)
        second = swap_blocks(rows[4:], COLS)
        field = jnp.concatenate(
            [jnp.concatenate([first[a], second[a]], axis=1) for a in range(ROWS)], axis=0
        ).astype(BF16)
        parts = mm(trig_hi[...], field, 1, 1) + mm(trig_lo[...], field, 1, 1)
        blocks = swap_blocks([parts[at * LATS : (at + 1) * LATS] for at in range(PARTS)], GROUP)
        flat = send_far.at[far_at].reshape(FAR * ROWS, 128)
        for a in range(ROWS):
            for part in range(2):
                flat[pl.ds(part * LATS * ROWS + a, LATS, stride=ROWS), :] = blocks[a * 2 + part]
        start_far(far_at, False)

    def take_spectrum(far_at):
        flat = recv_far.at[far_at].reshape(FAR * ROWS, 128)
        return (flat[0:NLAT, :] + flat[NLAT : 2 * NLAT, :]).T

    def send_spectrum(far_at, field):
        flat = send_far.at[far_at].reshape(FAR * ROWS, 128)
        flat[0:NLAT, :] = field.T
        start_far(far_at, True)

    def to_grid(far_at, near_at):
        flat = recv_far.at[far_at].reshape(FAR * ROWS, 128)
        rows = []
        for a in range(ROWS):
            for part in range(2):
                rows.append(flat[pl.ds(part * LATS * ROWS + a, LATS, stride=ROWS), :])
        stacked = jnp.concatenate(swap_blocks(rows, GROUP), axis=0).astype(BF16)
        field = mm(stacked, trig_hi[...], 0, 0) + mm(stacked, trig_lo[...], 0, 0)
        for side in range(2):
            blocks = swap_blocks(
                [
                    field[a * COLS : (a + 1) * COLS, side * 128 : (side + 1) * 128]
                    for a in range(ROWS)
                ],
                COLS,
            )
            for at in range(4):
                send_near[near_at, side * 4 + at] = blocks[at].astype(BF16)
        start_near(near_at)

    def analyse(rows, at):
        rows = rows.astype(BF16)
        return mm(rows, leg_hi[at], 1, 1) + mm(rows, leg_lo[at], 1, 1)

    def synthesise(rows, at):
        rows = rows.astype(BF16)
        return mm(rows, leg_hi[at]) + mm(rows, leg_lo[at])

    def order_weight(at):
        return jnp.where(lat * ORDERS + at == 0, 1.0, 2.0).astype(F32)

    xt = x_ref[...].astype(F32).T
    normed, inverse_in = layer_norm(xt)
    xt_v[...] = xt
    normed_v[...] = normed
    pl.semaphore_wait(barrier, NEAR - 1 + FAR - 1)
    send_field(0, normed)

    loads[0].wait()
    trig_hi[...], trig_lo[...] = split(trig_v[...])
    loads[1].wait()
    lat_at = lax.broadcasted_iota(jnp.int32, (TAPS, 128), 1)
    shift = lax.broadcasted_iota(jnp.int32, (TAPS, 128), 0) - REACH
    for r in range(TAPS):
        west, east = (ext_ref[r, 0:1, :], ext_ref[r, 1:2, :])
        inside = (shift >= -west) & (shift <= east)
        inside = inside & (lat_at + (r - REACH) >= 0) & (lat_at + (r - REACH) < NLAT)
        for k in range(BASIS):
            kept = jnp.where(inside, basis_ref[k, r].astype(F32), 0.0)
            total = phase_v[0] * kept[0:1]
            for d in range(1, TAPS):
                total = total + phase_v[d] * kept[d : d + 1]
            taps_v[k, r] = total
    for copy in loads[2:]:
        copy.wait()

    wait_near(0)
    to_spectrum(0, 0)

    leg_hi[...], leg_lo[...] = split(leg_v[...])
    mix = mix_v[...].reshape(BASIS * GROUP, GROUP)
    cott = cot_ref[...].astype(F32).T
    cott_v[...] = cott
    dhid_v[...] = mm(wout_v[...], cott.astype(BF16))
    wint_v[...] = win_v[...].T
    woutt_v[...] = wout_v[...].T
    quad = quad_ref[0:1, :]
    filter_real, filter_imag = (filt_ref[0], filt_ref[1])

    wait_far(0)
    spectrum = take_spectrum(0)
    for at in range(ORDERS):
        real = spectrum[at * 32 : at * 32 + 16]
        imag = spectrum[at * 32 + 16 : at * 32 + 32]
        sum_real = jnp.zeros((BASIS, GROUP, 128), F32)
        sum_imag = jnp.zeros((BASIS, GROUP, 128), F32)
        for r in range(TAPS):
            moved_real = pltpu.roll(real, (REACH - r) % 128, 1)[None]
            moved_imag = pltpu.roll(imag, (REACH - r) % 128, 1)[None]
            tap_real = taps_v[:, r, 2 * at : 2 * at + 1, :]
            tap_imag = taps_v[:, r, 2 * at + 1 : 2 * at + 2, :]
            sum_real = sum_real + (tap_real * moved_real - tap_imag * moved_imag)
            sum_imag = sum_imag + (tap_real * moved_imag + tap_imag * moved_real)
        conv_v[:, 2 * at * 128 : (2 * at + 1) * 128] = sum_real.reshape(144, 128).astype(BF16)
        conv_v[:, (2 * at + 1) * 128 : (2 * at + 2) * 128] = sum_imag.reshape(144, 128).astype(BF16)
    mixed = mm(mix, conv_v[...], 0, 0)
    pieces = []
    for at in range(ORDERS):
        rows = jnp.concatenate(
            [
                mixed[:, 2 * at * 128 : (2 * at + 1) * 128] * quad,
                mixed[:, (2 * at + 1) * 128 : (2 * at + 2) * 128] * quad,
            ],
            axis=0,
        )
        coefs = analyse(rows, at)
        coef_v[at] = coefs
        real, imag = (coefs[0:16], coefs[16:32])
        product = jnp.concatenate(
            [
                real * filter_real - imag * filter_imag,
                real * filter_imag + imag * filter_real,
            ],
            axis=0,
        )
        pieces.append(synthesise(product, at) * order_weight(at))
    send_spectrum(1, jnp.concatenate(pieces, axis=0))
    wait_far(1)
    to_grid(1, 1)
    wait_near(1)

    carried = xt_v[...] + take_field(1)
    normed_mid, inverse_mid = layer_norm(carried)
    preact = mm(wint_v[...], normed_mid.astype(BF16))
    bell = jnp.exp(-0.5 * preact * preact) * (1.0 / math.sqrt(2.0 * math.pi))
    gate = 0.5 * (1.0 + lax.erf(preact * (1.0 / math.sqrt(2.0))))
    d_preact = (dhid_v[...] * (gate + preact * bell)).astype(BF16)
    d_normed = mm(win_v[...], d_preact)
    d_carried = cott_v[...] + norm_back(normed_mid, inverse_mid, d_normed)
    send_field(2, d_carried)
    dcar_v[...] = d_carried
    hidden = (preact * gate).astype(BF16)
    output = carried + mm(woutt_v[...], hidden)
    out_ref[...] = output.T.astype(BF16)

    wait_near(2)
    to_spectrum(2, 2)
    wait_far(2)
    spectrum = take_spectrum(2)
    grad_real = jnp.zeros((GROUP, 128), F32)
    grad_imag = jnp.zeros((GROUP, 128), F32)
    pieces = []
    for at in range(ORDERS):
        upstream = analyse(spectrum[at * 32 : at * 32 + 32], at) * order_weight(at)
        up_real, up_imag = (upstream[0:16], upstream[16:32])
        real, imag = (coef_v[at, 0:16], coef_v[at, 16:32])
        grad_real = grad_real + (up_real * real + up_imag * imag)
        grad_imag = grad_imag + (up_imag * real - up_real * imag)
        d_coeff = jnp.concatenate(
            [
                up_real * filter_real + up_imag * filter_imag,
                up_imag * filter_real - up_real * filter_imag,
            ],
            axis=0,
        )
        rows = synthesise(d_coeff, at) * quad
        pieces.extend([rows[0:16], rows[16:32]])
    d_conv = mm(mix, jnp.concatenate(pieces, axis=1).astype(BF16))
    pieces = []
    for at in range(ORDERS):
        real = d_conv[:, 2 * at * 128 : (2 * at + 1) * 128].reshape(BASIS, GROUP, 128)
        imag = d_conv[:, (2 * at + 1) * 128 : (2 * at + 2) * 128].reshape(BASIS, GROUP, 128)
        sum_real = jnp.zeros((GROUP, 128), F32)
        sum_imag = jnp.zeros((GROUP, 128), F32)
        for r in range(TAPS):
            tap_real = taps_v[:, r, 2 * at : 2 * at + 1, :]
            tap_imag = taps_v[:, r, 2 * at + 1 : 2 * at + 2, :]
            row_real = jnp.sum(tap_real * real + tap_imag * imag, axis=0)
            row_imag = jnp.sum(tap_real * imag - tap_imag * real, axis=0)
            sum_real = sum_real + pltpu.roll(row_real, (r - REACH) % 128, 1)
            sum_imag = sum_imag + pltpu.roll(row_imag, (r - REACH) % 128, 1)
        pieces.extend([sum_real, sum_imag])
    send_spectrum(3, jnp.concatenate(pieces, axis=0))

    flat = grad_send.reshape(2 * GROUP, 128)
    flat[0:GROUP, :] = grad_real
    flat[GROUP : 2 * GROUP, :] = grad_imag

    def column_peer(step):
        peer = lax.rem(lat + 1 + step, LATS)
        return (peer, (peer, lon))

    def scatter(step):
        peer, device = column_peer(step)
        pltpu.make_async_remote_copy(
            src_ref=grad_send.at[peer],
            dst_ref=grad_recv.at[lat],
            send_sem=send_sem.at[8],
            recv_sem=recv_sem.at[8],
            device_id=device,
            device_id_type=MESH,
        ).start()

    def gather(step):
        peer, device = column_peer(step)
        pltpu.make_async_remote_copy(
            src_ref=grad_row.at[0],
            dst_ref=grad_all.at[lat],
            send_sem=send_sem.at[9],
            recv_sem=recv_sem.at[9],
            device_id=device,
            device_id_type=MESH,
        ).start()

    loop(LATS - 1, scatter)
    grad_recv[lat] = grad_send[lat]

    wait_far(3)
    to_grid(3, 3)

    block = grad_recv.at[pl.ds(0, LATS - 1)]
    pltpu.make_async_copy(block, block, recv_sem.at[8]).wait()
    grad_row[0] = jnp.sum(grad_recv[...], axis=0)
    loop(LATS - 1, gather)
    grad_all[lat] = grad_row[0]

    wait_near(3)
    d_normed_in = take_field(3)
    grad_x = dcar_v[...] + norm_back(normed_v[...], inverse_in, d_normed_in)
    gx_ref[...] = grad_x.T.astype(BF16)

    block = grad_all.at[pl.ds(0, LATS - 1)]
    pltpu.make_async_copy(block, block, recv_sem.at[9]).wait()
    gf_ref[...] = grad_all.reshape(2 * GROUP, 128)[...]

    for at in range(4):
        block = send_near.at[at, pl.ds(0, NEAR - 1)]
        pltpu.make_async_copy(block, block, send_sem.at[at]).wait()
        block = send_far.at[at, pl.ds(0, FAR - 1)]
        pltpu.make_async_copy(block, block, send_sem.at[4 + at]).wait()
    block = grad_send.at[pl.ds(0, LATS - 1)]
    pltpu.make_async_copy(block, block, send_sem.at[8]).wait()
    pltpu.make_async_copy(block, block, send_sem.at[9]).wait()


def local(activations, basis_weights, extents, mix_weight, spec_filter, w_in, w_out, cotangent):
    cells = ROWS * COLS
    vmem = pl.BlockSpec(memory_space=pltpu.VMEM)
    anywhere = pl.BlockSpec(memory_space=pl.ANY)
    out, grad_x, grad_filter = pl.pallas_call(
        body,
        out_shape=(
            jax.ShapeDtypeStruct((cells, CHANS), BF16),
            jax.ShapeDtypeStruct((cells, CHANS), BF16),
            jax.ShapeDtypeStruct((2 * GROUP, 128), F32),
        ),
        in_specs=[vmem] * 6 + [anywhere] * 6,
        out_specs=(vmem, vmem, vmem),
        scratch_shapes=[
            pltpu.VMEM((4, NEAR, 2 * GROUP, 128), BF16),
            pltpu.VMEM((4, NEAR, 2 * GROUP, 128), BF16),
            pltpu.VMEM((4, FAR, ROWS, 128), F32),
            pltpu.VMEM((4, FAR, ROWS, 128), F32),
            pltpu.VMEM((LATS, 1, 128), F32),
            pltpu.VMEM((LATS, 1, 128), F32),
            pltpu.VMEM((1, 1, 128), F32),
            pltpu.VMEM((LATS, 1, 128), F32),
            pltpu.VMEM((BASIS, GROUP, GROUP), BF16),
            pltpu.VMEM((CHANS, HIDDEN), BF16),
            pltpu.VMEM((HIDDEN, CHANS), BF16),
            pltpu.VMEM((ORDERS, NLAT, NLAT), F32),
            pltpu.VMEM((ORDERS, NLAT, NLAT), BF16),
            pltpu.VMEM((ORDERS, NLAT, NLAT), BF16),
            pltpu.VMEM((PARTS * LATS, NEAR * COLS), F32),
            pltpu.VMEM((PARTS * LATS, NEAR * COLS), BF16),
            pltpu.VMEM((PARTS * LATS, NEAR * COLS), BF16),
            pltpu.VMEM((TAPS, PARTS, 128), F32),
            pltpu.VMEM((BASIS, TAPS, PARTS, 128), F32),
            pltpu.VMEM((CHANS, cells), F32),
            pltpu.VMEM((CHANS, cells), F32),
            pltpu.VMEM((CHANS, cells), F32),
            pltpu.VMEM((HIDDEN, cells), F32),
            pltpu.VMEM((HIDDEN, CHANS), BF16),
            pltpu.VMEM((CHANS, HIDDEN), BF16),
            pltpu.VMEM((BASIS * GROUP, 2 * ORDERS * 128), BF16),
            pltpu.VMEM((ORDERS, 2 * GROUP, 128), F32),
            pltpu.VMEM((CHANS, cells), F32),
            pltpu.SemaphoreType.DMA((6,)),
            pltpu.SemaphoreType.DMA((10,)),
            pltpu.SemaphoreType.DMA((10,)),
        ],
        compiler_params=pltpu.CompilerParams(
            collective_id=0, has_side_effects=True, vmem_limit_bytes=48 * 1024 * 1024
        ),
        name="block",
    )(
        activations.reshape(cells, CHANS),
        cotangent.reshape(cells, CHANS),
        jnp.transpose(basis_weights, (0, 2, 3, 1)),
        jnp.transpose(extents, (2, 0, 1)),
        spec_filter,
        quad_values(),
        mix_weight,
        w_in,
        w_out,
        legendre_values(),
        trig_values(),
        phase_values(),
    )
    return (
        out.reshape(ROWS, COLS, CHANS),
        grad_x.reshape(ROWS, COLS, CHANS),
        grad_filter.reshape(2, GROUP, 128),
    )


def solution(mesh):
    placed = (
        P("lat", "lon", None),
        P(),
        P(),
        P(),
        P(None, "lon", None),
        P(),
        P(),
        P("lat", "lon", None),
    )
    return jax.shard_map(
        local,
        mesh=mesh,
        in_specs=placed,
        out_specs=(P("lat", "lon", None), P("lat", "lon", None), P(None, "lon", None)),
        check_vma=False,
    )
```

```python
import math

import jax
import jax.numpy as jnp
import numpy as np
from jax import lax
from jax.experimental import pallas as pl
from jax.experimental.pallas import tpu as pltpu
from jax.sharding import PartitionSpec as P

EPSILON = 1e-05
MESH = pl.DeviceIdType.MESH
F32 = jnp.float32
BF16 = jnp.bfloat16

NLAT = 128
NLON = 512
CHANS = 256
HIDDEN = 512
BASIS = 9
GROUP = 16
TAPS = 7
REACH = 3
LATS = 32
ROWS = 4
COLS = 32
ORDERS = 4
PARTS = 8
NEAR = 8
FAR = 64
FARTHEST = (4, 3, 5, 2, 6, 1, 7, 0)


def legendre_values():
    theta = math.pi * (np.arange(NLAT) + 0.5) / NLAT
    cosine, sine = (np.cos(theta), np.sin(theta))
    table = np.zeros((NLAT, NLAT, NLAT))
    for order in range(NLAT):
        steps = np.arange(1, order + 1)
        growth = np.sum(0.5 * np.log((2.0 * steps + 1.0) / (2.0 * steps)))
        earlier = np.zeros(NLAT)
        latest = np.exp(-0.5 * math.log(4.0 * math.pi) + growth + order * np.log(sine))
        table[order, order] = latest
        for degree in range(order + 1, NLAT):
            upper = math.sqrt((4.0 * degree**2 - 1.0) / (degree**2 - order**2))
            below = degree - 1.0
            lower = math.sqrt((below**2 - order**2) / (4.0 * below**2 - 1.0))
            earlier, latest = (latest, upper * (cosine * latest - lower * earlier))
            table[order, degree] = latest
    return table.astype(np.float32).reshape(LATS, ORDERS, NLAT, NLAT)


def trig_values():
    table = np.zeros((2, ORDERS, 2, LATS, NEAR, COLS))
    order = 4 * np.arange(LATS)[None, :] + np.arange(ORDERS)[:, None]
    for half in range(2):
        for near in range(NEAR):
            lon = 32 * ((near // 2) * 4 + half * 2 + near % 2) + np.arange(COLS)
            angle = (order[:, :, None] * lon[None, None, :] % NLON) * (2.0 * math.pi / NLON)
            table[half, :, 0, :, near] = np.cos(angle)
            table[half, :, 1, :, near] = -np.sin(angle)
    return table.astype(np.float32).reshape(2, PARTS * LATS, NEAR * COLS)


def phase_values():
    order = 4 * np.arange(LATS)[:, None] + np.arange(ORDERS)[None, :]
    shift = np.arange(TAPS) - REACH
    angle = order[:, None, :] * shift[None, :, None] * (2.0 * math.pi / NLON)
    pairs = np.stack([np.cos(angle), np.sin(angle)], axis=-1).reshape(LATS, TAPS, PARTS, 1)
    return np.broadcast_to(pairs, (LATS, TAPS, PARTS, 128)).astype(np.float32).copy()


def quad_values():
    theta = math.pi * (np.arange(NLAT) + 0.5) / NLAT
    weights = (2.0 * math.pi / NLON) * (math.pi / NLAT) * np.sin(theta)
    return np.broadcast_to(weights[None], (8, NLAT)).astype(np.float32).copy()


def mm(left, right, left_dim=1, right_dim=0):
    return lax.dot_general(
        left, right, (((left_dim,), (right_dim,)), ((), ())), preferred_element_type=F32
    )


def split(values):
    high = values.astype(BF16)
    return (high, (values - high.astype(F32)).astype(BF16))


def swap_blocks(blocks, width):
    blocks = list(blocks)
    lane = lax.broadcasted_iota(jnp.int32, blocks[0].shape, 1)
    stride = 1
    while stride < len(blocks):
        keep = (lane & (stride * width)) == 0
        for at in range(len(blocks)):
            if at & stride == 0:
                low, high = (blocks[at], blocks[at | stride])
                blocks[at] = jnp.where(keep, low, pltpu.roll(high, stride * width, 1))
                blocks[at | stride] = jnp.where(keep, pltpu.roll(low, 128 - stride * width, 1), high)
        stride *= 2
    return blocks


def layer_norm(values):
    centred = values - jnp.mean(values, axis=0, keepdims=True)
    inverse = lax.rsqrt(jnp.mean(centred * centred, axis=0, keepdims=True) + EPSILON)
    return (centred * inverse, inverse)


def norm_back(normed, inverse, upstream):
    return inverse * (
        upstream
        - jnp.mean(upstream, axis=0, keepdims=True)
        - normed * jnp.mean(upstream * normed, axis=0, keepdims=True)
    )


def near_of(group):
    return ((group // 4) * 2 + group % 2, (group // 2) % 2)


def body(
    x_hbm,
    cot_hbm,
    basis_hbm,
    ext_hbm,
    filt_hbm,
    mix_hbm,
    win_hbm,
    wout_hbm,
    leg_hbm,
    trig_hbm,
    phase_hbm,
    quad_hbm,
    out_ref,
    gx_ref,
    gf_ref,
    send_near,
    recv_near,
    send_far,
    recv_far,
    grad_send,
    grad_recv,
    grad_row,
    grad_all,
    mix_v,
    win_v,
    wout_v,
    leg_v,
    leg_hi,
    leg_lo,
    trig_v,
    trig_hi,
    trig_lo,
    phase_v,
    taps_v,
    xt_v,
    normed_v,
    cott_v,
    dhid_v,
    wint_v,
    woutt_v,
    conv_v,
    coef_v,
    dcar_v,
    x_ref,
    cot_ref,
    basis_ref,
    ext_ref,
    filt_ref,
    quad_ref,
    load_sem,
    ring_sem,
    send_sem,
    recv_sem,
):
    lat = lax.axis_index("lat")
    lon = lax.axis_index("lon")
    x_at, half, core = (lon // 4, lax.rem(lon // 2, 2), lax.rem(lon, 2))
    near_me = x_at * 2 + core
    far_me = half * LATS + lat
    z_me, y_me = (far_me // 8, lax.rem(far_me, 8))

    loads = []
    for index, (source, target) in enumerate(
        (
            (x_hbm, x_ref),
            (ext_hbm, ext_ref),
            (basis_hbm, basis_ref),
            (trig_hbm.at[half], trig_v),
            (phase_hbm.at[lat], phase_v),
            (leg_hbm.at[lat], leg_v),
            (mix_hbm.at[:, lon], mix_v),
            (win_hbm, win_v),
            (wout_hbm, wout_v),
            (cot_hbm, cot_ref),
            (filt_hbm, filt_ref),
            (quad_hbm, quad_ref),
        )
    ):
        copy = pltpu.make_async_copy(source, target, load_sem.at[index])
        copy.start()
        loads.append(copy)

    def near_peer(step):
        step = step + (step >= 4).astype(jnp.int32)
        peer = lax.rem(near_me + 4 + step, NEAR)
        return (peer, (lat, (peer // 2) * 4 + half * 2 + lax.rem(peer, 2)))

    def loop(count, action):
        def run(step, carry):
            action(step)
            return carry

        lax.fori_loop(0, count, run, 0)

    far_y = [lax.rem(y_me + move, 8) for move in FARTHEST]

    def far_device(peer_z, peer_y):
        peer_lat = lax.rem(peer_z, 4) * 8 + peer_y
        peer_lon = x_at * 4 + (peer_z // 4) * 2 + core
        return (peer_z * 8 + peer_y, peer_lat, (peer_lat, peer_lon))

    def over_far(action):
        def plane(step):
            away = (step + 1) // 2
            peer_z = lax.rem(z_me + 4 + away * (1 - 2 * lax.rem(step, 2)), 8)
            for peer_y in far_y:
                action(*far_device(peer_z, peer_y))

        loop(7, plane)
        for peer_y in far_y[:-1]:
            action(*far_device(z_me, peer_y))

    def ring_z(move):
        return far_device(lax.rem(z_me + move, 8), y_me)[2]

    barrier = pltpu.get_barrier_semaphore()

    def greet(device):
        pl.semaphore_signal(barrier, inc=1, device_id=device, device_id_type=MESH)

    for move in FARTHEST[:-1]:
        greet(ring_z(move))
    for peer_y in far_y[:-1]:
        greet(far_device(z_me, peer_y)[2])
    loop(NEAR - 1, lambda step: greet(near_peer(step)[1]))

    def start_near(at):
        def action(step):
            peer, device = near_peer(step)
            pltpu.make_async_remote_copy(
                src_ref=send_near.at[at, peer],
                dst_ref=recv_near.at[at, near_me],
                send_sem=send_sem.at[at],
                recv_sem=recv_sem.at[at],
                device_id=device,
                device_id_type=MESH,
            ).start()

        loop(NEAR - 1, action)
        recv_near[at, near_me] = send_near[at, near_me]

    def wait_near(at):
        block = recv_near.at[at, pl.ds(0, NEAR - 1)]
        pltpu.make_async_copy(block, block, recv_sem.at[at]).wait()

    def start_far(at, both):
        def action(peer, peer_lat, device):
            pltpu.make_async_remote_copy(
                src_ref=send_far.at[at, peer_lat if both else peer],
                dst_ref=recv_far.at[at, far_me],
                send_sem=send_sem.at[4 + at],
                recv_sem=recv_sem.at[4 + at],
                device_id=device,
                device_id_type=MESH,
            ).start()

        over_far(action)
        recv_far[at, far_me] = send_far[at, lat if both else far_me]

    def wait_far(at):
        block = recv_far.at[at, pl.ds(0, FAR - 1)]
        pltpu.make_async_copy(block, block, recv_sem.at[4 + at]).wait()

    def send_field(at, field):
        for group in range(CHANS // GROUP):
            near, part = near_of(group)
            send_near[at, near, part * GROUP : (part + 1) * GROUP, :] = field[
                group * GROUP : (group + 1) * GROUP
            ].astype(BF16)
        start_near(at)

    def take_field(at):
        pieces = []
        for group in range(CHANS // GROUP):
            near, part = near_of(group)
            pieces.append(recv_near[at, near, part * GROUP : (part + 1) * GROUP, :].astype(F32))
        return jnp.concatenate(pieces, axis=0)

    def to_spectrum(near_at, far_at):
        rows = [recv_near[near_at, near].astype(F32) for near in range(NEAR)]
        first = swap_blocks(rows[:4], COLS)
        second = swap_blocks(rows[4:], COLS)
        field = jnp.concatenate(
            [jnp.concatenate([first[a], second[a]], axis=1) for a in range(ROWS)], axis=0
        ).astype(BF16)
        parts = mm(trig_hi[...], field, 1, 1) + mm(trig_lo[...], field, 1, 1)
        blocks = swap_blocks([parts[at * LATS : (at + 1) * LATS] for at in range(PARTS)], GROUP)
        flat = send_far.at[far_at].reshape(FAR * ROWS, 128)
        for a in range(ROWS):
            for part in range(2):
                flat[pl.ds(part * LATS * ROWS + a, LATS, stride=ROWS), :] = blocks[a * 2 + part]
        if far_at == 0:
            pl.semaphore_wait(ring_sem, 7)
        start_far(far_at, False)

    def take_spectrum(far_at):
        flat = recv_far.at[far_at].reshape(FAR * ROWS, 128)
        return (flat[0:NLAT, :] + flat[NLAT : 2 * NLAT, :]).T

    def send_spectrum(far_at, field):
        flat = send_far.at[far_at].reshape(FAR * ROWS, 128)
        flat[0:NLAT, :] = field.T
        start_far(far_at, True)

    def to_grid(far_at, near_at):
        flat = recv_far.at[far_at].reshape(FAR * ROWS, 128)
        rows = []
        for a in range(ROWS):
            for part in range(2):
                rows.append(flat[pl.ds(part * LATS * ROWS + a, LATS, stride=ROWS), :])
        stacked = jnp.concatenate(swap_blocks(rows, GROUP), axis=0).astype(BF16)
        field = mm(stacked, trig_hi[...], 0, 0) + mm(stacked, trig_lo[...], 0, 0)
        for side in range(2):
            blocks = swap_blocks(
                [
                    field[a * COLS : (a + 1) * COLS, side * 128 : (side + 1) * 128]
                    for a in range(ROWS)
                ],
                COLS,
            )
            for at in range(4):
                send_near[near_at, side * 4 + at] = blocks[at].astype(BF16)
        start_near(near_at)

    def analyse(rows, at):
        rows = rows.astype(BF16)
        return mm(rows, leg_hi[at], 1, 1) + mm(rows, leg_lo[at], 1, 1)

    def synthesise(rows, at):
        rows = rows.astype(BF16)
        return mm(rows, leg_hi[at]) + mm(rows, leg_lo[at])

    def order_weight(at):
        return jnp.where(lat * ORDERS + at == 0, 1.0, 2.0).astype(F32)

    loads[0].wait()
    xt = x_ref[...].astype(F32).T
    normed, inverse_in = layer_norm(xt)
    xt_v[...] = xt
    normed_v[...] = normed
    pl.semaphore_wait(barrier, NEAR - 1 + 7 + 7)
    for move in FARTHEST[:-1]:
        pl.semaphore_signal(ring_sem, inc=1, device_id=ring_z(move), device_id_type=MESH)
    send_field(0, normed)

    for copy in loads[1:5]:
        copy.wait()
    trig_hi[...], trig_lo[...] = split(trig_v[...])
    lat_at = lax.broadcasted_iota(jnp.int32, (TAPS, 128), 1)
    shift = lax.broadcasted_iota(jnp.int32, (TAPS, 128), 0) - REACH
    for r in range(TAPS):
        west, east = (ext_ref[r, 0:1, :], ext_ref[r, 1:2, :])
        inside = (shift >= -west) & (shift <= east)
        inside = inside & (lat_at + (r - REACH) >= 0) & (lat_at + (r - REACH) < NLAT)
        for k in range(BASIS):
            kept = jnp.where(inside, basis_ref[k, r].astype(F32), 0.0)
            total = phase_v[0] * kept[0:1]
            for d in range(1, TAPS):
                total = total + phase_v[d] * kept[d : d + 1]
            taps_v[k, r] = total
    for copy in loads[5:]:
        copy.wait()

    wait_near(0)
    to_spectrum(0, 0)

    leg_hi[...], leg_lo[...] = split(leg_v[...])
    mix = mix_v[...].reshape(BASIS * GROUP, GROUP)
    cott = cot_ref[...].astype(F32).T
    cott_v[...] = cott
    dhid_v[...] = mm(wout_v[...], cott.astype(BF16))
    wint_v[...] = win_v[...].T
    woutt_v[...] = wout_v[...].T
    quad = quad_ref[0:1, :]
    filter_real, filter_imag = (filt_ref[0], filt_ref[1])

    wait_far(0)
    spectrum = take_spectrum(0)
    for at in range(ORDERS):
        real = spectrum[at * 32 : at * 32 + 16]
        imag = spectrum[at * 32 + 16 : at * 32 + 32]
        sum_real = jnp.zeros((BASIS, GROUP, 128), F32)
        sum_imag = jnp.zeros((BASIS, GROUP, 128), F32)
        for r in range(TAPS):
            moved_real = pltpu.roll(real, (REACH - r) % 128, 1)[None]
            moved_imag = pltpu.roll(imag, (REACH - r) % 128, 1)[None]
            tap_real = taps_v[:, r, 2 * at : 2 * at + 1, :]
            tap_imag = taps_v[:, r, 2 * at + 1 : 2 * at + 2, :]
            sum_real = sum_real + (tap_real * moved_real - tap_imag * moved_imag)
            sum_imag = sum_imag + (tap_real * moved_imag + tap_imag * moved_real)
        conv_v[:, 2 * at * 128 : (2 * at + 1) * 128] = sum_real.reshape(144, 128).astype(BF16)
        conv_v[:, (2 * at + 1) * 128 : (2 * at + 2) * 128] = sum_imag.reshape(144, 128).astype(BF16)
    mixed = mm(mix, conv_v[...], 0, 0)
    pieces = []
    for at in range(ORDERS):
        rows = jnp.concatenate(
            [
                mixed[:, 2 * at * 128 : (2 * at + 1) * 128] * quad,
                mixed[:, (2 * at + 1) * 128 : (2 * at + 2) * 128] * quad,
            ],
            axis=0,
        )
        coefs = analyse(rows, at)
        coef_v[at] = coefs
        real, imag = (coefs[0:16], coefs[16:32])
        product = jnp.concatenate(
            [
                real * filter_real - imag * filter_imag,
                real * filter_imag + imag * filter_real,
            ],
            axis=0,
        )
        pieces.append(synthesise(product, at) * order_weight(at))
    send_spectrum(1, jnp.concatenate(pieces, axis=0))
    wait_far(1)
    to_grid(1, 1)
    wait_near(1)

    carried = xt_v[...] + take_field(1)
    normed_mid, inverse_mid = layer_norm(carried)
    preact = mm(wint_v[...], normed_mid.astype(BF16))
    bell = jnp.exp(-0.5 * preact * preact) * (1.0 / math.sqrt(2.0 * math.pi))
    gate = 0.5 * (1.0 + lax.erf(preact * (1.0 / math.sqrt(2.0))))
    d_preact = (dhid_v[...] * (gate + preact * bell)).astype(BF16)
    d_normed = mm(win_v[...], d_preact)
    d_carried = cott_v[...] + norm_back(normed_mid, inverse_mid, d_normed)
    send_field(2, d_carried)
    dcar_v[...] = d_carried
    hidden = (preact * gate).astype(BF16)
    output = carried + mm(woutt_v[...], hidden)
    out_ref[...] = output.T.astype(BF16)

    wait_near(2)
    to_spectrum(2, 2)
    wait_far(2)
    spectrum = take_spectrum(2)
    grad_real = jnp.zeros((GROUP, 128), F32)
    grad_imag = jnp.zeros((GROUP, 128), F32)
    pieces = []
    for at in range(ORDERS):
        upstream = analyse(spectrum[at * 32 : at * 32 + 32], at) * order_weight(at)
        up_real, up_imag = (upstream[0:16], upstream[16:32])
        real, imag = (coef_v[at, 0:16], coef_v[at, 16:32])
        grad_real = grad_real + (up_real * real + up_imag * imag)
        grad_imag = grad_imag + (up_imag * real - up_real * imag)
        d_coeff = jnp.concatenate(
            [
                up_real * filter_real + up_imag * filter_imag,
                up_imag * filter_real - up_real * filter_imag,
            ],
            axis=0,
        )
        rows = synthesise(d_coeff, at) * quad
        pieces.extend([rows[0:16], rows[16:32]])
    d_conv = mm(mix, jnp.concatenate(pieces, axis=1).astype(BF16))
    pieces = []
    for at in range(ORDERS):
        real = d_conv[:, 2 * at * 128 : (2 * at + 1) * 128].reshape(BASIS, GROUP, 128)
        imag = d_conv[:, (2 * at + 1) * 128 : (2 * at + 2) * 128].reshape(BASIS, GROUP, 128)
        sum_real = jnp.zeros((GROUP, 128), F32)
        sum_imag = jnp.zeros((GROUP, 128), F32)
        for r in range(TAPS):
            tap_real = taps_v[:, r, 2 * at : 2 * at + 1, :]
            tap_imag = taps_v[:, r, 2 * at + 1 : 2 * at + 2, :]
            row_real = jnp.sum(tap_real * real + tap_imag * imag, axis=0)
            row_imag = jnp.sum(tap_real * imag - tap_imag * real, axis=0)
            sum_real = sum_real + pltpu.roll(row_real, (r - REACH) % 128, 1)
            sum_imag = sum_imag + pltpu.roll(row_imag, (r - REACH) % 128, 1)
        pieces.extend([sum_real, sum_imag])
    send_spectrum(3, jnp.concatenate(pieces, axis=0))

    flat = grad_send.reshape(2 * GROUP, 128)
    flat[0:GROUP, :] = grad_real
    flat[GROUP : 2 * GROUP, :] = grad_imag

    def column_peer(step):
        peer = lax.rem(lat + 1 + step, LATS)
        return (peer, (peer, lon))

    def scatter(step):
        peer, device = column_peer(step)
        pltpu.make_async_remote_copy(
            src_ref=grad_send.at[peer],
            dst_ref=grad_recv.at[lat],
            send_sem=send_sem.at[8],
            recv_sem=recv_sem.at[8],
            device_id=device,
            device_id_type=MESH,
        ).start()

    def gather(step):
        peer, device = column_peer(step)
        pltpu.make_async_remote_copy(
            src_ref=grad_row.at[0],
            dst_ref=grad_all.at[lat],
            send_sem=send_sem.at[9],
            recv_sem=recv_sem.at[9],
            device_id=device,
            device_id_type=MESH,
        ).start()

    loop(LATS - 1, scatter)
    grad_recv[lat] = grad_send[lat]

    wait_far(3)
    to_grid(3, 3)

    block = grad_recv.at[pl.ds(0, LATS - 1)]
    pltpu.make_async_copy(block, block, recv_sem.at[8]).wait()
    grad_row[0] = jnp.sum(grad_recv[...], axis=0)
    loop(LATS - 1, gather)
    grad_all[lat] = grad_row[0]

    wait_near(3)
    d_normed_in = take_field(3)
    grad_x = dcar_v[...] + norm_back(normed_v[...], inverse_in, d_normed_in)
    gx_ref[...] = grad_x.T.astype(BF16)

    block = grad_all.at[pl.ds(0, LATS - 1)]
    pltpu.make_async_copy(block, block, recv_sem.at[9]).wait()
    gf_ref[...] = grad_all.reshape(2 * GROUP, 128)[...]

    for at in range(4):
        block = send_near.at[at, pl.ds(0, NEAR - 1)]
        pltpu.make_async_copy(block, block, send_sem.at[at]).wait()
        block = send_far.at[at, pl.ds(0, FAR - 1)]
        pltpu.make_async_copy(block, block, send_sem.at[4 + at]).wait()
    block = grad_send.at[pl.ds(0, LATS - 1)]
    pltpu.make_async_copy(block, block, send_sem.at[8]).wait()
    pltpu.make_async_copy(block, block, send_sem.at[9]).wait()


def local(activations, basis_weights, extents, mix_weight, spec_filter, w_in, w_out, cotangent):
    cells = ROWS * COLS
    vmem = pl.BlockSpec(memory_space=pltpu.VMEM)
    hbm = pl.BlockSpec(memory_space=pltpu.HBM)
    out, grad_x, grad_filter = pl.pallas_call(
        body,
        out_shape=(
            jax.ShapeDtypeStruct((cells, CHANS), BF16),
            jax.ShapeDtypeStruct((cells, CHANS), BF16),
            jax.ShapeDtypeStruct((2 * GROUP, 128), F32),
        ),
        in_specs=[hbm] * 12,
        out_specs=(vmem, vmem, vmem),
        scratch_shapes=[
            pltpu.VMEM((4, NEAR, 2 * GROUP, 128), BF16),
            pltpu.VMEM((4, NEAR, 2 * GROUP, 128), BF16),
            pltpu.VMEM((4, FAR, ROWS, 128), F32),
            pltpu.VMEM((4, FAR, ROWS, 128), F32),
            pltpu.VMEM((LATS, 1, 128), F32),
            pltpu.VMEM((LATS, 1, 128), F32),
            pltpu.VMEM((1, 1, 128), F32),
            pltpu.VMEM((LATS, 1, 128), F32),
            pltpu.VMEM((BASIS, GROUP, GROUP), BF16),
            pltpu.VMEM((CHANS, HIDDEN), BF16),
            pltpu.VMEM((HIDDEN, CHANS), BF16),
            pltpu.VMEM((ORDERS, NLAT, NLAT), F32),
            pltpu.VMEM((ORDERS, NLAT, NLAT), BF16),
            pltpu.VMEM((ORDERS, NLAT, NLAT), BF16),
            pltpu.VMEM((PARTS * LATS, NEAR * COLS), F32),
            pltpu.VMEM((PARTS * LATS, NEAR * COLS), BF16),
            pltpu.VMEM((PARTS * LATS, NEAR * COLS), BF16),
            pltpu.VMEM((TAPS, PARTS, 128), F32),
            pltpu.VMEM((BASIS, TAPS, PARTS, 128), F32),
            pltpu.VMEM((CHANS, cells), F32),
            pltpu.VMEM((CHANS, cells), F32),
            pltpu.VMEM((CHANS, cells), F32),
            pltpu.VMEM((HIDDEN, cells), F32),
            pltpu.VMEM((HIDDEN, CHANS), BF16),
            pltpu.VMEM((CHANS, HIDDEN), BF16),
            pltpu.VMEM((BASIS * GROUP, 2 * ORDERS * 128), BF16),
            pltpu.VMEM((ORDERS, 2 * GROUP, 128), F32),
            pltpu.VMEM((CHANS, cells), F32),
            pltpu.VMEM((cells, CHANS), BF16),
            pltpu.VMEM((cells, CHANS), BF16),
            pltpu.VMEM((BASIS, TAPS, TAPS, NLAT), BF16),
            pltpu.VMEM((TAPS, 2, NLAT), jnp.int32),
            pltpu.VMEM((2, GROUP, NLAT), F32),
            pltpu.VMEM((8, NLAT), F32),
            pltpu.SemaphoreType.DMA((12,)),
            pltpu.SemaphoreType.REGULAR,
            pltpu.SemaphoreType.DMA((10,)),
            pltpu.SemaphoreType.DMA((10,)),
        ],
        compiler_params=pltpu.CompilerParams(
            collective_id=0, has_side_effects=True, vmem_limit_bytes=60 * 1024 * 1024
        ),
        name="block",
    )(
        activations.reshape(cells, CHANS),
        cotangent.reshape(cells, CHANS),
        jnp.transpose(basis_weights, (0, 2, 3, 1)),
        jnp.transpose(extents, (2, 0, 1)),
        spec_filter,
        mix_weight,
        w_in,
        w_out,
        legendre_values(),
        trig_values(),
        phase_values(),
        quad_values(),
    )
    return (
        out.reshape(ROWS, COLS, CHANS),
        grad_x.reshape(ROWS, COLS, CHANS),
        grad_filter.reshape(2, GROUP, 128),
    )


def solution(mesh):
    placed = (
        P("lat", "lon", None),
        P(),
        P(),
        P(),
        P(None, "lon", None),
        P(),
        P(),
        P("lat", "lon", None),
    )
    return jax.shard_map(
        local,
        mesh=mesh,
        in_specs=placed,
        out_specs=(P("lat", "lon", None), P("lat", "lon", None), P(None, "lon", None)),
        check_vma=False,
    )
```

```python
import math

import jax
import jax.numpy as jnp
import numpy as np
from jax import lax
from jax.experimental import pallas as pl
from jax.experimental.pallas import tpu as pltpu
from jax.sharding import PartitionSpec as P

EPSILON = 1e-05
MESH = pl.DeviceIdType.MESH
F32 = jnp.float32
BF16 = jnp.bfloat16

NLAT = 128
NLON = 512
CHANS = 256
HIDDEN = 512
BASIS = 9
GROUP = 16
TAPS = 7
REACH = 3
LATS = 32
ROWS = 4
COLS = 32
ORDERS = 4
PARTS = 8
NEAR = 8
FAR = 64
FARTHEST = (4, 3, 5, 2, 6, 1, 7, 0)


def legendre_values():
    theta = math.pi * (np.arange(NLAT) + 0.5) / NLAT
    cosine, sine = (np.cos(theta), np.sin(theta))
    table = np.zeros((NLAT, NLAT, NLAT))
    for order in range(NLAT):
        steps = np.arange(1, order + 1)
        growth = np.sum(0.5 * np.log((2.0 * steps + 1.0) / (2.0 * steps)))
        earlier = np.zeros(NLAT)
        latest = np.exp(-0.5 * math.log(4.0 * math.pi) + growth + order * np.log(sine))
        table[order, order] = latest
        for degree in range(order + 1, NLAT):
            upper = math.sqrt((4.0 * degree**2 - 1.0) / (degree**2 - order**2))
            below = degree - 1.0
            lower = math.sqrt((below**2 - order**2) / (4.0 * below**2 - 1.0))
            earlier, latest = (latest, upper * (cosine * latest - lower * earlier))
            table[order, degree] = latest
    return table.astype(np.float32).reshape(LATS, ORDERS, NLAT, NLAT)


def trig_values():
    table = np.zeros((2, ORDERS, 2, LATS, NEAR, COLS))
    order = 4 * np.arange(LATS)[None, :] + np.arange(ORDERS)[:, None]
    for half in range(2):
        for near in range(NEAR):
            lon = 32 * ((near // 2) * 4 + half * 2 + near % 2) + np.arange(COLS)
            angle = (order[:, :, None] * lon[None, None, :] % NLON) * (2.0 * math.pi / NLON)
            table[half, :, 0, :, near] = np.cos(angle)
            table[half, :, 1, :, near] = -np.sin(angle)
    return table.astype(np.float32).reshape(2, PARTS * LATS, NEAR * COLS)


def phase_values():
    order = 4 * np.arange(LATS)[:, None] + np.arange(ORDERS)[None, :]
    shift = np.arange(TAPS) - REACH
    angle = order[:, None, :] * shift[None, :, None] * (2.0 * math.pi / NLON)
    pairs = np.stack([np.cos(angle), np.sin(angle)], axis=-1).reshape(LATS, TAPS, PARTS, 1)
    return np.broadcast_to(pairs, (LATS, TAPS, PARTS, 128)).astype(np.float32).copy()


def quad_values():
    theta = math.pi * (np.arange(NLAT) + 0.5) / NLAT
    weights = (2.0 * math.pi / NLON) * (math.pi / NLAT) * np.sin(theta)
    return np.broadcast_to(weights[None], (8, NLAT)).astype(np.float32).copy()


def mm(left, right, left_dim=1, right_dim=0):
    return lax.dot_general(
        left, right, (((left_dim,), (right_dim,)), ((), ())), preferred_element_type=F32
    )


def split(values):
    high = values.astype(BF16)
    return (high, (values - high.astype(F32)).astype(BF16))


def swap_blocks(blocks, width):
    blocks = list(blocks)
    lane = lax.broadcasted_iota(jnp.int32, blocks[0].shape, 1)
    stride = 1
    while stride < len(blocks):
        keep = (lane & (stride * width)) == 0
        for at in range(len(blocks)):
            if at & stride == 0:
                low, high = (blocks[at], blocks[at | stride])
                blocks[at] = jnp.where(keep, low, pltpu.roll(high, stride * width, 1))
                blocks[at | stride] = jnp.where(keep, pltpu.roll(low, 128 - stride * width, 1), high)
        stride *= 2
    return blocks


def layer_norm(values):
    centred = values - jnp.mean(values, axis=0, keepdims=True)
    inverse = lax.rsqrt(jnp.mean(centred * centred, axis=0, keepdims=True) + EPSILON)
    return (centred * inverse, inverse)


def norm_back(normed, inverse, upstream):
    return inverse * (
        upstream
        - jnp.mean(upstream, axis=0, keepdims=True)
        - normed * jnp.mean(upstream * normed, axis=0, keepdims=True)
    )


def near_of(group):
    return ((group // 4) * 2 + group % 2, (group // 2) % 2)


def body(
    x_hbm,
    cot_hbm,
    basis_hbm,
    ext_hbm,
    filt_hbm,
    mix_hbm,
    win_hbm,
    wout_hbm,
    leg_hbm,
    trig_hbm,
    phase_hbm,
    quad_hbm,
    out_hbm,
    gx_hbm,
    gf_hbm,
    send_near,
    recv_near,
    send_far,
    recv_far,
    grad_send,
    grad_recv,
    grad_row,
    grad_all,
    mix_v,
    win_v,
    wout_v,
    leg_v,
    leg_in,
    leg_out,
    trig_v,
    trig_down,
    trig_wide,
    phase_v,
    taps_v,
    xt_v,
    normed_v,
    cott_v,
    dhid_v,
    wint_v,
    woutt_v,
    conv_v,
    coef_v,
    dcar_v,
    x_ref,
    cot_ref,
    basis_ref,
    ext_ref,
    filt_ref,
    quad_ref,
    out_ref,
    gx_ref,
    gf_ref,
    load_sem,
    store_sem,
    ring_sem,
    send_sem,
    recv_sem,
):
    lat = lax.axis_index("lat")
    lon = lax.axis_index("lon")
    x_at, half, core = (lon // 4, lax.rem(lon // 2, 2), lax.rem(lon, 2))
    near_me = x_at * 2 + core
    far_me = half * LATS + lat
    z_me, y_me = (far_me // 8, lax.rem(far_me, 8))

    loads = []
    for index, (source, target) in enumerate(
        (
            (x_hbm, x_ref),
            (ext_hbm, ext_ref),
            (basis_hbm, basis_ref),
            (trig_hbm.at[half], trig_v),
            (phase_hbm.at[lat], phase_v),
            (leg_hbm.at[lat], leg_v),
            (mix_hbm.at[:, lon], mix_v),
            (win_hbm, win_v),
            (wout_hbm, wout_v),
            (cot_hbm, cot_ref),
            (filt_hbm, filt_ref),
            (quad_hbm, quad_ref),
        )
    ):
        copy = pltpu.make_async_copy(source, target, load_sem.at[index])
        copy.start()
        loads.append(copy)

    def near_peer(step):
        step = step + (step >= 4).astype(jnp.int32)
        peer = lax.rem(near_me + 4 + step, NEAR)
        return (peer, (lat, (peer // 2) * 4 + half * 2 + lax.rem(peer, 2)))

    def loop(count, action):
        def run(step, carry):
            action(step)
            return carry

        lax.fori_loop(0, count, run, 0)

    far_y = [lax.rem(y_me + move, 8) for move in FARTHEST]

    def far_device(peer_z, peer_y):
        peer_lat = lax.rem(peer_z, 4) * 8 + peer_y
        peer_lon = x_at * 4 + (peer_z // 4) * 2 + core
        return (peer_z * 8 + peer_y, peer_lat, (peer_lat, peer_lon))

    def over_far(action):
        def plane(step):
            away = (step + 1) // 2
            peer_z = lax.rem(z_me + 4 + away * (1 - 2 * lax.rem(step, 2)), 8)
            for peer_y in far_y:
                action(*far_device(peer_z, peer_y))

        loop(7, plane)
        for peer_y in far_y[:-1]:
            action(*far_device(z_me, peer_y))

    def ring_z(move):
        return far_device(lax.rem(z_me + move, 8), y_me)[2]

    barrier = pltpu.get_barrier_semaphore()

    def greet(device):
        pl.semaphore_signal(barrier, inc=1, device_id=device, device_id_type=MESH)

    for move in FARTHEST[:-1]:
        greet(ring_z(move))
    for peer_y in far_y[:-1]:
        greet(far_device(z_me, peer_y)[2])
    loop(NEAR - 1, lambda step: greet(near_peer(step)[1]))

    def start_near(at):
        def action(step):
            peer, device = near_peer(step)
            pltpu.make_async_remote_copy(
                src_ref=send_near.at[at, peer],
                dst_ref=recv_near.at[at, near_me],
                send_sem=send_sem.at[at],
                recv_sem=recv_sem.at[at],
                device_id=device,
                device_id_type=MESH,
            ).start()

        loop(NEAR - 1, action)
        recv_near[at, near_me] = send_near[at, near_me]

    def wait_near(at):
        block = recv_near.at[at, pl.ds(0, NEAR - 1)]
        pltpu.make_async_copy(block, block, recv_sem.at[at]).wait()

    def start_far(at, both):
        def action(peer, peer_lat, device):
            pltpu.make_async_remote_copy(
                src_ref=send_far.at[at, peer_lat if both else peer],
                dst_ref=recv_far.at[at, far_me],
                send_sem=send_sem.at[4 + at],
                recv_sem=recv_sem.at[4 + at],
                device_id=device,
                device_id_type=MESH,
            ).start()

        over_far(action)
        recv_far[at, far_me] = send_far[at, lat if both else far_me]

    def wait_far(at):
        block = recv_far.at[at, pl.ds(0, FAR - 1)]
        pltpu.make_async_copy(block, block, recv_sem.at[4 + at]).wait()

    def send_field(at, field):
        for group in range(CHANS // GROUP):
            near, part = near_of(group)
            send_near[at, near, part * GROUP : (part + 1) * GROUP, :] = field[
                group * GROUP : (group + 1) * GROUP
            ].astype(BF16)
        start_near(at)

    def take_field(at):
        pieces = []
        for group in range(CHANS // GROUP):
            near, part = near_of(group)
            pieces.append(recv_near[at, near, part * GROUP : (part + 1) * GROUP, :].astype(F32))
        return jnp.concatenate(pieces, axis=0)

    def to_spectrum(near_at, far_at):
        rows = [recv_near[near_at, near].astype(F32) for near in range(NEAR)]
        first = swap_blocks(rows[:4], COLS)
        second = swap_blocks(rows[4:], COLS)
        field = jnp.concatenate(
            [jnp.concatenate([first[a], second[a]], axis=1) for a in range(ROWS)], axis=0
        ).astype(BF16)
        parts = mm(trig_down[...], field, 1, 1)
        parts = parts[0 : PARTS * LATS] + parts[PARTS * LATS :]
        blocks = swap_blocks([parts[at * LATS : (at + 1) * LATS] for at in range(PARTS)], GROUP)
        flat = send_far.at[far_at].reshape(FAR * ROWS, 128)
        for a in range(ROWS):
            for part in range(2):
                flat[pl.ds(part * LATS * ROWS + a, LATS, stride=ROWS), :] = blocks[a * 2 + part]
        if far_at == 0:
            pl.semaphore_wait(ring_sem, 7)
        start_far(far_at, False)

    def take_spectrum(far_at):
        flat = recv_far.at[far_at].reshape(FAR * ROWS, 128)
        return (flat[0:NLAT, :] + flat[NLAT : 2 * NLAT, :]).T

    def send_spectrum(far_at, field):
        flat = send_far.at[far_at].reshape(FAR * ROWS, 128)
        flat[0:NLAT, :] = field.T
        start_far(far_at, True)

    def to_grid(far_at, near_at):
        flat = recv_far.at[far_at].reshape(FAR * ROWS, 128)
        rows = []
        for a in range(ROWS):
            for part in range(2):
                rows.append(flat[pl.ds(part * LATS * ROWS + a, LATS, stride=ROWS), :])
        stacked = jnp.concatenate(swap_blocks(rows, GROUP), axis=0).astype(BF16)
        field = mm(stacked, trig_wide[...], 0, 0)
        field = field[:, 0 : NEAR * COLS] + field[:, NEAR * COLS :]
        for side in range(2):
            blocks = swap_blocks(
                [
                    field[a * COLS : (a + 1) * COLS, side * 128 : (side + 1) * 128]
                    for a in range(ROWS)
                ],
                COLS,
            )
            for at in range(4):
                send_near[near_at, side * 4 + at] = blocks[at].astype(BF16)
        start_near(near_at)

    def analyse(rows, at):
        both = mm(rows.astype(BF16), leg_in[at])
        return both[:, 0:NLAT] + both[:, NLAT:]

    def synthesise(rows, at):
        both = mm(rows.astype(BF16), leg_out[at])
        return both[:, 0:NLAT] + both[:, NLAT:]

    def order_weight(at):
        return jnp.where(lat * ORDERS + at == 0, 1.0, 2.0).astype(F32)

    loads[0].wait()
    xt = x_ref[...].astype(F32).T
    normed, inverse_in = layer_norm(xt)
    xt_v[...] = xt
    normed_v[...] = normed
    pl.semaphore_wait(barrier, NEAR - 1 + 7 + 7)
    send_field(0, normed)
    for move in FARTHEST[:-1]:
        pl.semaphore_signal(ring_sem, inc=1, device_id=ring_z(move), device_id_type=MESH)

    for copy in loads[1:5]:
        copy.wait()
    high, low = split(trig_v[...])
    trig_down[0 : PARTS * LATS] = high
    trig_down[PARTS * LATS :] = low
    trig_wide[:, 0 : NEAR * COLS] = high
    trig_wide[:, NEAR * COLS :] = low
    lat_at = lax.broadcasted_iota(jnp.int32, (TAPS, 128), 1)
    shift = lax.broadcasted_iota(jnp.int32, (TAPS, 128), 0) - REACH
    for r in range(TAPS):
        west, east = (ext_ref[r, 0:1, :], ext_ref[r, 1:2, :])
        inside = (shift >= -west) & (shift <= east)
        inside = inside & (lat_at + (r - REACH) >= 0) & (lat_at + (r - REACH) < NLAT)
        for k in range(BASIS):
            kept = jnp.where(inside, basis_ref[k, r].astype(F32), 0.0)
            total = phase_v[0] * kept[0:1]
            for d in range(1, TAPS):
                total = total + phase_v[d] * kept[d : d + 1]
            taps_v[k, r] = total
    for copy in loads[5:]:
        copy.wait()

    wait_near(0)
    to_spectrum(0, 0)

    for at in range(ORDERS):
        high, low = split(leg_v[at])
        leg_out[at, :, 0:NLAT] = high
        leg_out[at, :, NLAT:] = low
        high, low = split(leg_v[at].T)
        leg_in[at, :, 0:NLAT] = high
        leg_in[at, :, NLAT:] = low
    mix = mix_v[...].reshape(BASIS * GROUP, GROUP)
    cott = cot_ref[...].astype(F32).T
    cott_v[...] = cott
    dhid_v[...] = mm(wout_v[...], cott.astype(BF16))
    wint_v[...] = win_v[...].T
    woutt_v[...] = wout_v[...].T
    quad = quad_ref[0:1, :]
    filter_real, filter_imag = (filt_ref[0], filt_ref[1])

    wait_far(0)
    spectrum = take_spectrum(0)
    for at in range(ORDERS):
        real = spectrum[at * 32 : at * 32 + 16]
        imag = spectrum[at * 32 + 16 : at * 32 + 32]
        sum_real = jnp.zeros((BASIS, GROUP, 128), F32)
        sum_imag = jnp.zeros((BASIS, GROUP, 128), F32)
        for r in range(TAPS):
            moved_real = pltpu.roll(real, (REACH - r) % 128, 1)[None]
            moved_imag = pltpu.roll(imag, (REACH - r) % 128, 1)[None]
            tap_real = taps_v[:, r, 2 * at : 2 * at + 1, :]
            tap_imag = taps_v[:, r, 2 * at + 1 : 2 * at + 2, :]
            sum_real = sum_real + (tap_real * moved_real - tap_imag * moved_imag)
            sum_imag = sum_imag + (tap_real * moved_imag + tap_imag * moved_real)
        conv_v[:, 2 * at * 128 : (2 * at + 1) * 128] = sum_real.reshape(144, 128).astype(BF16)
        conv_v[:, (2 * at + 1) * 128 : (2 * at + 2) * 128] = sum_imag.reshape(144, 128).astype(BF16)
    mixed = mm(mix, conv_v[...], 0, 0)
    pieces = []
    for at in range(ORDERS):
        rows = jnp.concatenate(
            [
                mixed[:, 2 * at * 128 : (2 * at + 1) * 128] * quad,
                mixed[:, (2 * at + 1) * 128 : (2 * at + 2) * 128] * quad,
            ],
            axis=0,
        )
        coefs = analyse(rows, at)
        coef_v[at] = coefs
        real, imag = (coefs[0:16], coefs[16:32])
        product = jnp.concatenate(
            [
                real * filter_real - imag * filter_imag,
                real * filter_imag + imag * filter_real,
            ],
            axis=0,
        )
        pieces.append(synthesise(product, at) * order_weight(at))
    send_spectrum(1, jnp.concatenate(pieces, axis=0))
    wait_far(1)
    to_grid(1, 1)
    wait_near(1)

    carried = xt_v[...] + take_field(1)
    normed_mid, inverse_mid = layer_norm(carried)
    preact = mm(wint_v[...], normed_mid.astype(BF16))
    bell = jnp.exp(-0.5 * preact * preact) * (1.0 / math.sqrt(2.0 * math.pi))
    gate = 0.5 * (1.0 + lax.erf(preact * (1.0 / math.sqrt(2.0))))
    d_preact = (dhid_v[...] * (gate + preact * bell)).astype(BF16)
    d_normed = mm(win_v[...], d_preact)
    d_carried = cott_v[...] + norm_back(normed_mid, inverse_mid, d_normed)
    send_field(2, d_carried)
    dcar_v[...] = d_carried
    hidden = (preact * gate).astype(BF16)
    output = carried + mm(woutt_v[...], hidden)
    out_ref[...] = output.T.astype(BF16)
    store_out = pltpu.make_async_copy(out_ref, out_hbm, store_sem.at[0])
    store_out.start()

    wait_near(2)
    to_spectrum(2, 2)
    wait_far(2)
    spectrum = take_spectrum(2)
    grad_real = jnp.zeros((GROUP, 128), F32)
    grad_imag = jnp.zeros((GROUP, 128), F32)
    upstreams = []
    for at in range(ORDERS):
        upstream = analyse(spectrum[at * 32 : at * 32 + 32], at) * order_weight(at)
        up_real, up_imag = (upstream[0:16], upstream[16:32])
        upstreams.append((up_real, up_imag))
        real, imag = (coef_v[at, 0:16], coef_v[at, 16:32])
        grad_real = grad_real + (up_real * real + up_imag * imag)
        grad_imag = grad_imag + (up_imag * real - up_real * imag)

    flat = grad_send.reshape(2 * GROUP, 128)
    flat[0:GROUP, :] = grad_real
    flat[GROUP : 2 * GROUP, :] = grad_imag

    def column_peer(step):
        peer = lax.rem(lat + 1 + step, LATS)
        return (peer, (peer, lon))

    def scatter(step):
        peer, device = column_peer(step)
        pltpu.make_async_remote_copy(
            src_ref=grad_send.at[peer],
            dst_ref=grad_recv.at[lat],
            send_sem=send_sem.at[8],
            recv_sem=recv_sem.at[8],
            device_id=device,
            device_id_type=MESH,
        ).start()

    def gather(step):
        peer, device = column_peer(step)
        pltpu.make_async_remote_copy(
            src_ref=grad_row.at[0],
            dst_ref=grad_all.at[lat],
            send_sem=send_sem.at[9],
            recv_sem=recv_sem.at[9],
            device_id=device,
            device_id_type=MESH,
        ).start()

    loop(LATS - 1, scatter)
    grad_recv[lat] = grad_send[lat]

    pieces = []
    for at in range(ORDERS):
        up_real, up_imag = upstreams[at]
        d_coeff = jnp.concatenate(
            [
                up_real * filter_real + up_imag * filter_imag,
                up_imag * filter_real - up_real * filter_imag,
            ],
            axis=0,
        )
        rows = synthesise(d_coeff, at) * quad
        pieces.extend([rows[0:16], rows[16:32]])
    d_conv = mm(mix, jnp.concatenate(pieces, axis=1).astype(BF16))
    pieces = []
    for at in range(ORDERS):
        real = d_conv[:, 2 * at * 128 : (2 * at + 1) * 128].reshape(BASIS, GROUP, 128)
        imag = d_conv[:, (2 * at + 1) * 128 : (2 * at + 2) * 128].reshape(BASIS, GROUP, 128)
        sum_real = jnp.zeros((GROUP, 128), F32)
        sum_imag = jnp.zeros((GROUP, 128), F32)
        for r in range(TAPS):
            tap_real = taps_v[:, r, 2 * at : 2 * at + 1, :]
            tap_imag = taps_v[:, r, 2 * at + 1 : 2 * at + 2, :]
            row_real = jnp.sum(tap_real * real + tap_imag * imag, axis=0)
            row_imag = jnp.sum(tap_real * imag - tap_imag * real, axis=0)
            sum_real = sum_real + pltpu.roll(row_real, (r - REACH) % 128, 1)
            sum_imag = sum_imag + pltpu.roll(row_imag, (r - REACH) % 128, 1)
        pieces.extend([sum_real, sum_imag])
    send_spectrum(3, jnp.concatenate(pieces, axis=0))

    block = grad_recv.at[pl.ds(0, LATS - 1)]
    pltpu.make_async_copy(block, block, recv_sem.at[8]).wait()
    grad_row[0] = jnp.sum(grad_recv[...], axis=0)
    loop(LATS - 1, gather)
    grad_all[lat] = grad_row[0]

    wait_far(3)
    to_grid(3, 3)

    wait_near(3)
    d_normed_in = take_field(3)
    grad_x = dcar_v[...] + norm_back(normed_v[...], inverse_in, d_normed_in)
    gx_ref[...] = grad_x.T.astype(BF16)
    store_gx = pltpu.make_async_copy(gx_ref, gx_hbm, store_sem.at[1])
    store_gx.start()

    block = grad_all.at[pl.ds(0, LATS - 1)]
    pltpu.make_async_copy(block, block, recv_sem.at[9]).wait()
    gf_ref[...] = grad_all.reshape(2 * GROUP, 128)[...]
    store_gf = pltpu.make_async_copy(gf_ref, gf_hbm, store_sem.at[2])
    store_gf.start()

    for at in range(4):
        block = send_near.at[at, pl.ds(0, NEAR - 1)]
        pltpu.make_async_copy(block, block, send_sem.at[at]).wait()
        block = send_far.at[at, pl.ds(0, FAR - 1)]
        pltpu.make_async_copy(block, block, send_sem.at[4 + at]).wait()
    block = grad_send.at[pl.ds(0, LATS - 1)]
    pltpu.make_async_copy(block, block, send_sem.at[8]).wait()
    pltpu.make_async_copy(block, block, send_sem.at[9]).wait()
    store_out.wait()
    store_gx.wait()
    store_gf.wait()


def hand_out(first, second, third, first_out, second_out, third_out):
    first_out[...] = first[...]
    second_out[...] = second[...]
    third_out[...] = third[...]


def local(activations, basis_weights, extents, mix_weight, spec_filter, w_in, w_out, cotangent):
    cells = ROWS * COLS
    vmem = pl.BlockSpec(memory_space=pltpu.VMEM)
    hbm = pl.BlockSpec(memory_space=pltpu.HBM)
    out, grad_x, grad_filter = pl.pallas_call(
        body,
        out_shape=(
            jax.ShapeDtypeStruct((cells, CHANS), BF16),
            jax.ShapeDtypeStruct((cells, CHANS), BF16),
            jax.ShapeDtypeStruct((2 * GROUP, 128), F32),
        ),
        in_specs=[hbm] * 12,
        out_specs=(hbm, hbm, hbm),
        scratch_shapes=[
            pltpu.VMEM((4, NEAR, 2 * GROUP, 128), BF16),
            pltpu.VMEM((4, NEAR, 2 * GROUP, 128), BF16),
            pltpu.VMEM((4, FAR, ROWS, 128), F32),
            pltpu.VMEM((4, FAR, ROWS, 128), F32),
            pltpu.VMEM((LATS, 1, 128), F32),
            pltpu.VMEM((LATS, 1, 128), F32),
            pltpu.VMEM((1, 1, 128), F32),
            pltpu.VMEM((LATS, 1, 128), F32),
            pltpu.VMEM((BASIS, GROUP, GROUP), BF16),
            pltpu.VMEM((CHANS, HIDDEN), BF16),
            pltpu.VMEM((HIDDEN, CHANS), BF16),
            pltpu.VMEM((ORDERS, NLAT, NLAT), F32),
            pltpu.VMEM((ORDERS, NLAT, 2 * NLAT), BF16),
            pltpu.VMEM((ORDERS, NLAT, 2 * NLAT), BF16),
            pltpu.VMEM((PARTS * LATS, NEAR * COLS), F32),
            pltpu.VMEM((2 * PARTS * LATS, NEAR * COLS), BF16),
            pltpu.VMEM((PARTS * LATS, 2 * NEAR * COLS), BF16),
            pltpu.VMEM((TAPS, PARTS, 128), F32),
            pltpu.VMEM((BASIS, TAPS, PARTS, 128), F32),
            pltpu.VMEM((CHANS, cells), F32),
            pltpu.VMEM((CHANS, cells), F32),
            pltpu.VMEM((CHANS, cells), F32),
            pltpu.VMEM((HIDDEN, cells), F32),
            pltpu.VMEM((HIDDEN, CHANS), BF16),
            pltpu.VMEM((CHANS, HIDDEN), BF16),
            pltpu.VMEM((BASIS * GROUP, 2 * ORDERS * 128), BF16),
            pltpu.VMEM((ORDERS, 2 * GROUP, 128), F32),
            pltpu.VMEM((CHANS, cells), F32),
            pltpu.VMEM((cells, CHANS), BF16),
            pltpu.VMEM((cells, CHANS), BF16),
            pltpu.VMEM((BASIS, TAPS, TAPS, NLAT), BF16),
            pltpu.VMEM((TAPS, 2, NLAT), jnp.int32),
            pltpu.VMEM((2, GROUP, NLAT), F32),
            pltpu.VMEM((8, NLAT), F32),
            pltpu.VMEM((cells, CHANS), BF16),
            pltpu.VMEM((cells, CHANS), BF16),
            pltpu.VMEM((2 * GROUP, 128), F32),
            pltpu.SemaphoreType.DMA((12,)),
            pltpu.SemaphoreType.DMA((3,)),
            pltpu.SemaphoreType.REGULAR,
            pltpu.SemaphoreType.DMA((10,)),
            pltpu.SemaphoreType.DMA((10,)),
        ],
        compiler_params=pltpu.CompilerParams(
            collective_id=0, has_side_effects=True, vmem_limit_bytes=60 * 1024 * 1024
        ),
        name="block",
    )(
        activations.reshape(cells, CHANS),
        cotangent.reshape(cells, CHANS),
        jnp.transpose(basis_weights, (0, 2, 3, 1)),
        jnp.transpose(extents, (2, 0, 1)),
        spec_filter,
        mix_weight,
        w_in,
        w_out,
        legendre_values(),
        trig_values(),
        phase_values(),
        quad_values(),
    )
    out, grad_x, grad_filter = pl.pallas_call(
        hand_out,
        out_shape=(
            jax.ShapeDtypeStruct((cells, CHANS), BF16),
            jax.ShapeDtypeStruct((cells, CHANS), BF16),
            jax.ShapeDtypeStruct((2 * GROUP, 128), F32),
        ),
        in_specs=[vmem] * 3,
        out_specs=(vmem,) * 3,
        name="hand_out",
    )(out, grad_x, grad_filter)
    return (
        out.reshape(ROWS, COLS, CHANS),
        grad_x.reshape(ROWS, COLS, CHANS),
        grad_filter.reshape(2, GROUP, 128),
    )


def solution(mesh):
    placed = (
        P("lat", "lon", None),
        P(),
        P(),
        P(),
        P(None, "lon", None),
        P(),
        P(),
        P("lat", "lon", None),
    )
    return jax.shard_map(
        local,
        mesh=mesh,
        in_specs=placed,
        out_specs=(P("lat", "lon", None), P("lat", "lon", None), P(None, "lon", None)),
        check_vma=False,
    )
```

```python
import math

import jax
import jax.numpy as jnp
import numpy as np
from jax import lax
from jax.experimental import pallas as pl
from jax.experimental.pallas import tpu as pltpu
from jax.sharding import PartitionSpec as P

EPSILON = 1e-05
MESH = pl.DeviceIdType.MESH
F32 = jnp.float32
BF16 = jnp.bfloat16

NLAT = 128
NLON = 512
CHANS = 256
HIDDEN = 512
BASIS = 9
GROUP = 16
TAPS = 7
REACH = 3
LATS = 32
ROWS = 4
COLS = 32
ORDERS = 4
PARTS = 8
NEAR = 8
FAR = 64
FIELD_STEPS = ((1, 16), (2, 64))
NEAREST = (4, 5, 3, 2, 6, 1, 7)
ORDER_STEPS = ((1, 16), (2, 32), (4, 64))
FARTHEST = (4, 3, 5, 2, 6, 1, 7, 0)


def legendre_values():
    theta = math.pi * (np.arange(NLAT) + 0.5) / NLAT
    cosine, sine = (np.cos(theta), np.sin(theta))
    table = np.zeros((NLAT, NLAT, NLAT))
    for order in range(NLAT):
        steps = np.arange(1, order + 1)
        growth = np.sum(0.5 * np.log((2.0 * steps + 1.0) / (2.0 * steps)))
        earlier = np.zeros(NLAT)
        latest = np.exp(-0.5 * math.log(4.0 * math.pi) + growth + order * np.log(sine))
        table[order, order] = latest
        for degree in range(order + 1, NLAT):
            upper = math.sqrt((4.0 * degree**2 - 1.0) / (degree**2 - order**2))
            below = degree - 1.0
            lower = math.sqrt((below**2 - order**2) / (4.0 * below**2 - 1.0))
            earlier, latest = (latest, upper * (cosine * latest - lower * earlier))
            table[order, degree] = latest
    return table.astype(np.float32).reshape(LATS, ORDERS, NLAT, NLAT)


def trig_values():
    table = np.zeros((2, ORDERS, 2, LATS, NEAR, COLS))
    order = 4 * np.arange(LATS)[None, :] + np.arange(ORDERS)[:, None]
    for half in range(2):
        for near in range(NEAR):
            lon = 32 * ((near // 2) * 4 + half * 2 + near % 2) + np.arange(COLS)
            angle = (order[:, :, None] * lon[None, None, :] % NLON) * (2.0 * math.pi / NLON)
            table[half, :, 0, :, near] = np.cos(angle)
            table[half, :, 1, :, near] = -np.sin(angle)
    return table.astype(np.float32).reshape(2, PARTS * LATS, NEAR * COLS)


def phase_values():
    order = 4 * np.arange(LATS)[:, None] + np.arange(ORDERS)[None, :]
    shift = np.arange(TAPS) - REACH
    angle = order[:, None, :] * shift[None, :, None] * (2.0 * math.pi / NLON)
    pairs = np.stack([np.cos(angle), np.sin(angle)], axis=-1).reshape(LATS, TAPS, PARTS, 1)
    return np.broadcast_to(pairs, (LATS, TAPS, PARTS, 128)).astype(np.float32).copy()


def quad_values():
    theta = math.pi * (np.arange(NLAT) + 0.5) / NLAT
    weights = (2.0 * math.pi / NLON) * (math.pi / NLAT) * np.sin(theta)
    return np.broadcast_to(weights[None], (8, NLAT)).astype(np.float32).copy()


def mm(left, right, left_dim=1, right_dim=0):
    return lax.dot_general(
        left, right, (((left_dim,), (right_dim,)), ((), ())), preferred_element_type=F32
    )


def split(values):
    high = values.astype(BF16)
    return (high, (values - high.astype(F32)).astype(BF16))


def swap_blocks(blocks, steps):
    blocks = list(blocks)
    lane = lax.broadcasted_iota(jnp.int32, blocks[0].shape, 1)
    for stride, width in steps:
        keep = (lane & width) == 0
        for at in range(len(blocks)):
            if at & stride == 0:
                low, high = (blocks[at], blocks[at | stride])
                blocks[at] = jnp.where(keep, low, pltpu.roll(high, width, 1))
                blocks[at | stride] = jnp.where(keep, pltpu.roll(low, 128 - width, 1), high)
    return blocks


def layer_norm(values):
    centred = values - jnp.mean(values, axis=1, keepdims=True)
    inverse = lax.rsqrt(jnp.mean(centred * centred, axis=1, keepdims=True) + EPSILON)
    return (centred * inverse, inverse)


def norm_back(normed, inverse, upstream):
    return inverse * (
        upstream
        - jnp.mean(upstream, axis=1, keepdims=True)
        - normed * jnp.mean(upstream * normed, axis=1, keepdims=True)
    )


def body(
    x_hbm,
    cot_hbm,
    basis_hbm,
    ext_hbm,
    filt_hbm,
    mix_hbm,
    win_hbm,
    wout_hbm,
    leg_hbm,
    trig_hbm,
    phase_hbm,
    quad_hbm,
    out_ref,
    gx_ref,
    gf_ref,
    send_near,
    recv_near,
    send_far,
    recv_far,
    grad_send,
    grad_recv,
    grad_row,
    grad_all,
    mix_v,
    win_v,
    wout_v,
    leg_v,
    leg_in,
    leg_out,
    trig_v,
    trig_down,
    trig_up,
    phase_v,
    taps_v,
    normed_v,
    dhid_v,
    wint_v,
    woutt_v,
    conv_v,
    coef_v,
    dcar_v,
    x_ref,
    cot_ref,
    basis_ref,
    ext_ref,
    filt_ref,
    quad_ref,
    load_sem,
    ring_sem,
    send_sem,
    recv_sem,
):
    lat = lax.axis_index("lat")
    lon = lax.axis_index("lon")
    x_at, half, core = (lon // 4, lax.rem(lon // 2, 2), lax.rem(lon, 2))
    near_me = x_at * 2 + core
    far_me = half * LATS + lat
    z_me, y_me = (far_me // 8, lax.rem(far_me, 8))

    def over_near(action):
        for move in NEAREST:
            peer = lax.rem(near_me + move, NEAR)
            action(peer, (lat, (peer // 2) * 4 + half * 2 + lax.rem(peer, 2)))

    def loop(count, action):
        def run(step, carry):
            action(step)
            return carry

        lax.fori_loop(0, count, run, 0)

    far_y = [lax.rem(y_me + move, 8) for move in FARTHEST]

    def far_device(peer_z, peer_y):
        peer_lat = lax.rem(peer_z, 4) * 8 + peer_y
        peer_lon = x_at * 4 + (peer_z // 4) * 2 + core
        return (peer_z * 8 + peer_y, peer_lat, (peer_lat, peer_lon))

    def over_far(action):
        def plane(step):
            away = (step + 1) // 2
            peer_z = lax.rem(z_me + 4 + away * (1 - 2 * lax.rem(step, 2)), 8)
            for peer_y in far_y:
                action(*far_device(peer_z, peer_y))

        loop(7, plane)
        for peer_y in far_y[:-1]:
            action(*far_device(z_me, peer_y))

    def ring_z(move):
        return far_device(lax.rem(z_me + move, 8), y_me)[2]

    barrier = pltpu.get_barrier_semaphore()

    def greet(device):
        pl.semaphore_signal(barrier, inc=1, device_id=device, device_id_type=MESH)

    over_near(lambda peer, device: greet(device))
    for move in FARTHEST[:-1]:
        greet(ring_z(move))
    for peer_y in far_y[:-1]:
        greet(far_device(z_me, peer_y)[2])

    loads = []
    for index, (source, target) in enumerate(
        (
            (x_hbm, x_ref),
            (ext_hbm, ext_ref),
            (basis_hbm, basis_ref),
            (trig_hbm.at[half], trig_v),
            (phase_hbm.at[lat], phase_v),
            (leg_hbm.at[lat], leg_v),
            (mix_hbm.at[:, lon], mix_v),
            (win_hbm, win_v),
            (wout_hbm, wout_v),
            (cot_hbm, cot_ref),
            (filt_hbm, filt_ref),
            (quad_hbm, quad_ref),
        )
    ):
        copy = pltpu.make_async_copy(source, target, load_sem.at[index])
        copy.start()
        loads.append(copy)

    def start_near(at):
        def action(peer, device):
            pltpu.make_async_remote_copy(
                src_ref=send_near.at[at, peer],
                dst_ref=recv_near.at[at, near_me],
                send_sem=send_sem.at[at],
                recv_sem=recv_sem.at[at],
                device_id=device,
                device_id_type=MESH,
            ).start()

        over_near(action)
        recv_near[at, near_me] = send_near[at, near_me]

    def wait_near(at):
        block = recv_near.at[at, pl.ds(0, NEAR - 1)]
        pltpu.make_async_copy(block, block, recv_sem.at[at]).wait()

    def start_far(at, both):
        def action(peer, peer_lat, device):
            pltpu.make_async_remote_copy(
                src_ref=send_far.at[at, peer_lat if both else peer],
                dst_ref=recv_far.at[at, far_me],
                send_sem=send_sem.at[4 + at],
                recv_sem=recv_sem.at[4 + at],
                device_id=device,
                device_id_type=MESH,
            ).start()

        over_far(action)
        recv_far[at, far_me] = send_far[at, lat if both else far_me]

    def wait_far(at):
        block = recv_far.at[at, pl.ds(0, FAR - 1)]
        pltpu.make_async_copy(block, block, recv_sem.at[4 + at]).wait()

    def fill_field(at, field):
        for side in range(2):
            blocks = swap_blocks(
                [
                    field[a * COLS : (a + 1) * COLS, side * 128 : (side + 1) * 128]
                    for a in range(ROWS)
                ],
                FIELD_STEPS,
            )
            for near in range(4):
                send_near[at, side * 4 + near] = blocks[near].astype(BF16)

    def take_field(at):
        sides = [
            jnp.concatenate(
                swap_blocks(
                    [recv_near[at, side * 4 + near].astype(F32) for near in range(4)], FIELD_STEPS
                ),
                axis=0,
            )
            for side in range(2)
        ]
        return jnp.concatenate(sides, axis=1)

    def spectrum_rows(flat, spot):
        row, part = (2 * (spot // 4) + spot % 2, spot // 2 % 2)
        return flat.at[pl.ds(part * LATS * ROWS + row, LATS, stride=ROWS), :]

    def to_spectrum(near_at, far_at):
        field = recv_near[near_at].reshape(NEAR * COLS, 128)
        parts = mm(trig_down[...], field)
        parts = parts[0 : PARTS * LATS] + parts[PARTS * LATS :]
        blocks = swap_blocks(
            [parts[at * LATS : (at + 1) * LATS] for at in range(PARTS)], ORDER_STEPS
        )
        flat = send_far.at[far_at].reshape(FAR * ROWS, 128)
        for spot in range(PARTS):
            spectrum_rows(flat, spot)[...] = blocks[spot]
        if far_at == 0:
            pl.semaphore_wait(ring_sem, 7)
        start_far(far_at, False)

    def take_spectrum(far_at):
        flat = recv_far.at[far_at].reshape(FAR * ROWS, 128)
        return (flat[0:NLAT, :] + flat[NLAT : 2 * NLAT, :]).T

    def send_spectrum(far_at, field):
        flat = send_far.at[far_at].reshape(FAR * ROWS, 128)
        flat[0:NLAT, :] = field.T
        start_far(far_at, True)

    def to_grid(far_at, near_at):
        flat = recv_far.at[far_at].reshape(FAR * ROWS, 128)
        rows = [spectrum_rows(flat, spot)[...] for spot in range(PARTS)]
        stacked = jnp.concatenate(swap_blocks(rows, ORDER_STEPS), axis=0).astype(BF16)
        field = mm(trig_up[...], stacked)
        field = (field[0 : NEAR * COLS] + field[NEAR * COLS :]).astype(BF16)
        send_near[near_at] = field.reshape(NEAR, COLS, 128)
        start_near(near_at)

    def analyse(rows, at):
        both = mm(rows.astype(BF16), leg_in[at])
        return both[:, 0:NLAT] + both[:, NLAT:]

    def synthesise(rows, at):
        both = mm(rows.astype(BF16), leg_out[at])
        return both[:, 0:NLAT] + both[:, NLAT:]

    def order_weight(at):
        return jnp.where(lat * ORDERS + at == 0, 1.0, 2.0).astype(F32)

    loads[0].wait()
    normed, inverse_in = layer_norm(x_ref[...].astype(F32))
    normed_v[...] = normed
    fill_field(0, normed)
    pl.semaphore_wait(barrier, NEAR - 1 + 7 + 7)
    start_near(0)
    for move in FARTHEST[:-1]:
        pl.semaphore_signal(ring_sem, inc=1, device_id=ring_z(move), device_id_type=MESH)

    for copy in loads[1:5]:
        copy.wait()
    high, low = split(trig_v[...])
    trig_down[0 : PARTS * LATS] = high
    trig_down[PARTS * LATS :] = low
    high, low = split(trig_v[...].T)
    trig_up[0 : NEAR * COLS] = high
    trig_up[NEAR * COLS :] = low
    lat_at = lax.broadcasted_iota(jnp.int32, (TAPS, 128), 1)
    shift = lax.broadcasted_iota(jnp.int32, (TAPS, 128), 0) - REACH
    for r in range(TAPS):
        west, east = (ext_ref[r, 0:1, :], ext_ref[r, 1:2, :])
        inside = (shift >= -west) & (shift <= east)
        inside = inside & (lat_at + (r - REACH) >= 0) & (lat_at + (r - REACH) < NLAT)
        for k in range(BASIS):
            kept = jnp.where(inside, basis_ref[k, r].astype(F32), 0.0)
            total = phase_v[0] * kept[0:1]
            for d in range(1, TAPS):
                total = total + phase_v[d] * kept[d : d + 1]
            taps_v[k, r] = total
    for copy in loads[5:]:
        copy.wait()

    wait_near(0)
    to_spectrum(0, 0)

    for at in range(ORDERS):
        high, low = split(leg_v[at])
        leg_out[at, :, 0:NLAT] = high
        leg_out[at, :, NLAT:] = low
        high, low = split(leg_v[at].T)
        leg_in[at, :, 0:NLAT] = high
        leg_in[at, :, NLAT:] = low
    mix = mix_v[...].reshape(BASIS * GROUP, GROUP)
    wint_v[...] = win_v[...].T
    woutt_v[...] = wout_v[...].T
    dhid_v[...] = mm(cot_ref[...], woutt_v[...])
    quad = quad_ref[0:1, :]
    filter_real, filter_imag = (filt_ref[0], filt_ref[1])

    wait_far(0)
    spectrum = take_spectrum(0)
    for at in range(ORDERS):
        real = spectrum[at * 32 : at * 32 + 16]
        imag = spectrum[at * 32 + 16 : at * 32 + 32]
        sum_real = jnp.zeros((BASIS, GROUP, 128), F32)
        sum_imag = jnp.zeros((BASIS, GROUP, 128), F32)
        for r in range(TAPS):
            moved_real = pltpu.roll(real, (REACH - r) % 128, 1)[None]
            moved_imag = pltpu.roll(imag, (REACH - r) % 128, 1)[None]
            tap_real = taps_v[:, r, 2 * at : 2 * at + 1, :]
            tap_imag = taps_v[:, r, 2 * at + 1 : 2 * at + 2, :]
            sum_real = sum_real + (tap_real * moved_real - tap_imag * moved_imag)
            sum_imag = sum_imag + (tap_real * moved_imag + tap_imag * moved_real)
        conv_v[:, 2 * at * 128 : (2 * at + 1) * 128] = sum_real.reshape(144, 128).astype(BF16)
        conv_v[:, (2 * at + 1) * 128 : (2 * at + 2) * 128] = sum_imag.reshape(144, 128).astype(BF16)
    mixed = mm(mix, conv_v[...], 0, 0)
    pieces = []
    for at in range(ORDERS):
        rows = jnp.concatenate(
            [
                mixed[:, 2 * at * 128 : (2 * at + 1) * 128] * quad,
                mixed[:, (2 * at + 1) * 128 : (2 * at + 2) * 128] * quad,
            ],
            axis=0,
        )
        coefs = analyse(rows, at)
        coef_v[at] = coefs
        real, imag = (coefs[0:16], coefs[16:32])
        product = jnp.concatenate(
            [
                real * filter_real - imag * filter_imag,
                real * filter_imag + imag * filter_real,
            ],
            axis=0,
        )
        pieces.append(synthesise(product, at) * order_weight(at))
    send_spectrum(1, jnp.concatenate(pieces, axis=0))
    wait_far(1)
    to_grid(1, 1)
    wait_near(1)

    carried = x_ref[...].astype(F32) + take_field(1)
    normed_mid, inverse_mid = layer_norm(carried)
    preact = mm(normed_mid.astype(BF16), win_v[...])
    bell = jnp.exp(-0.5 * preact * preact) * (1.0 / math.sqrt(2.0 * math.pi))
    gate = 0.5 * (1.0 + lax.erf(preact * (1.0 / math.sqrt(2.0))))
    d_preact = (dhid_v[...] * (gate + preact * bell)).astype(BF16)
    d_normed = mm(d_preact, wint_v[...])
    d_carried = cot_ref[...].astype(F32) + norm_back(normed_mid, inverse_mid, d_normed)
    fill_field(2, d_carried)
    start_near(2)
    dcar_v[...] = d_carried
    hidden = (preact * gate).astype(BF16)
    out_ref[...] = (carried + mm(hidden, wout_v[...])).astype(BF16)

    wait_near(2)
    to_spectrum(2, 2)
    wait_far(2)
    spectrum = take_spectrum(2)
    grad_real = jnp.zeros((GROUP, 128), F32)
    grad_imag = jnp.zeros((GROUP, 128), F32)
    upstreams = []
    for at in range(ORDERS):
        upstream = analyse(spectrum[at * 32 : at * 32 + 32], at) * order_weight(at)
        up_real, up_imag = (upstream[0:16], upstream[16:32])
        upstreams.append((up_real, up_imag))
        real, imag = (coef_v[at, 0:16], coef_v[at, 16:32])
        grad_real = grad_real + (up_real * real + up_imag * imag)
        grad_imag = grad_imag + (up_imag * real - up_real * imag)

    flat = grad_send.reshape(2 * GROUP, 128)
    flat[0:GROUP, :] = grad_real
    flat[GROUP : 2 * GROUP, :] = grad_imag

    def column_peer(step):
        peer = lax.rem(lat + 1 + step, LATS)
        return (peer, (peer, lon))

    def scatter(step):
        peer, device = column_peer(step)
        pltpu.make_async_remote_copy(
            src_ref=grad_send.at[peer],
            dst_ref=grad_recv.at[lat],
            send_sem=send_sem.at[8],
            recv_sem=recv_sem.at[8],
            device_id=device,
            device_id_type=MESH,
        ).start()

    def gather(step):
        peer, device = column_peer(step)
        pltpu.make_async_remote_copy(
            src_ref=grad_row.at[0],
            dst_ref=grad_all.at[lat],
            send_sem=send_sem.at[9],
            recv_sem=recv_sem.at[9],
            device_id=device,
            device_id_type=MESH,
        ).start()

    for step in range(LATS - 1):
        scatter(step)
    grad_recv[lat] = grad_send[lat]

    pieces = []
    for at in range(ORDERS):
        up_real, up_imag = upstreams[at]
        d_coeff = jnp.concatenate(
            [
                up_real * filter_real + up_imag * filter_imag,
                up_imag * filter_real - up_real * filter_imag,
            ],
            axis=0,
        )
        rows = synthesise(d_coeff, at) * quad
        pieces.extend([rows[0:16], rows[16:32]])
    d_conv = mm(mix, jnp.concatenate(pieces, axis=1).astype(BF16))
    pieces = []
    for at in range(ORDERS):
        real = d_conv[:, 2 * at * 128 : (2 * at + 1) * 128].reshape(BASIS, GROUP, 128)
        imag = d_conv[:, (2 * at + 1) * 128 : (2 * at + 2) * 128].reshape(BASIS, GROUP, 128)
        sum_real = jnp.zeros((GROUP, 128), F32)
        sum_imag = jnp.zeros((GROUP, 128), F32)
        for r in range(TAPS):
            tap_real = taps_v[:, r, 2 * at : 2 * at + 1, :]
            tap_imag = taps_v[:, r, 2 * at + 1 : 2 * at + 2, :]
            row_real = jnp.sum(tap_real * real + tap_imag * imag, axis=0)
            row_imag = jnp.sum(tap_real * imag - tap_imag * real, axis=0)
            sum_real = sum_real + pltpu.roll(row_real, (r - REACH) % 128, 1)
            sum_imag = sum_imag + pltpu.roll(row_imag, (r - REACH) % 128, 1)
        pieces.extend([sum_real, sum_imag])
    send_spectrum(3, jnp.concatenate(pieces, axis=0))

    block = grad_recv.at[pl.ds(0, LATS - 1)]
    pltpu.make_async_copy(block, block, recv_sem.at[8]).wait()
    grad_row[0] = jnp.sum(grad_recv[...], axis=0)
    loop(LATS - 1, gather)
    grad_all[lat] = grad_row[0]

    wait_far(3)
    to_grid(3, 3)

    wait_near(3)
    d_normed_in = take_field(3)
    grad_x = dcar_v[...] + norm_back(normed_v[...], inverse_in, d_normed_in)
    gx_ref[...] = grad_x.astype(BF16)

    block = grad_all.at[pl.ds(0, LATS - 1)]
    pltpu.make_async_copy(block, block, recv_sem.at[9]).wait()
    gf_ref[...] = grad_all.reshape(2 * GROUP, 128)[...]

    for at in range(4):
        block = send_near.at[at, pl.ds(0, NEAR - 1)]
        pltpu.make_async_copy(block, block, send_sem.at[at]).wait()
        block = send_far.at[at, pl.ds(0, FAR - 1)]
        pltpu.make_async_copy(block, block, send_sem.at[4 + at]).wait()
    block = grad_send.at[pl.ds(0, LATS - 1)]
    pltpu.make_async_copy(block, block, send_sem.at[8]).wait()
    pltpu.make_async_copy(block, block, send_sem.at[9]).wait()


def hand_out(first, second, third, first_out, second_out, third_out):
    first_out[...] = first[...]
    second_out[...] = second[...]
    third_out[...] = third[...]


def local(activations, basis_weights, extents, mix_weight, spec_filter, w_in, w_out, cotangent):
    cells = ROWS * COLS
    vmem = pl.BlockSpec(memory_space=pltpu.VMEM)
    hbm = pl.BlockSpec(memory_space=pltpu.HBM)
    out, grad_x, grad_filter = pl.pallas_call(
        body,
        out_shape=(
            pltpu.VMEM((cells, CHANS), BF16),
            pltpu.VMEM((cells, CHANS), BF16),
            pltpu.VMEM((2 * GROUP, 128), F32),
        ),
        in_specs=[hbm] * 12,
        out_specs=(vmem, vmem, vmem),
        scratch_shapes=[
            pltpu.VMEM((4, NEAR, 2 * GROUP, 128), BF16),
            pltpu.VMEM((4, NEAR, 2 * GROUP, 128), BF16),
            pltpu.VMEM((4, FAR, ROWS, 128), F32),
            pltpu.VMEM((4, FAR, ROWS, 128), F32),
            pltpu.VMEM((LATS, 1, 128), F32),
            pltpu.VMEM((LATS, 1, 128), F32),
            pltpu.VMEM((1, 1, 128), F32),
            pltpu.VMEM((LATS, 1, 128), F32),
            pltpu.VMEM((BASIS, GROUP, GROUP), BF16),
            pltpu.VMEM((CHANS, HIDDEN), BF16),
            pltpu.VMEM((HIDDEN, CHANS), BF16),
            pltpu.VMEM((ORDERS, NLAT, NLAT), F32),
            pltpu.VMEM((ORDERS, NLAT, 2 * NLAT), BF16),
            pltpu.VMEM((ORDERS, NLAT, 2 * NLAT), BF16),
            pltpu.VMEM((PARTS * LATS, NEAR * COLS), F32),
            pltpu.VMEM((2 * PARTS * LATS, NEAR * COLS), BF16),
            pltpu.VMEM((2 * NEAR * COLS, PARTS * LATS), BF16),
            pltpu.VMEM((TAPS, PARTS, 128), F32),
            pltpu.VMEM((BASIS, TAPS, PARTS, 128), F32),
            pltpu.VMEM((cells, CHANS), F32),
            pltpu.VMEM((cells, HIDDEN), F32),
            pltpu.VMEM((HIDDEN, CHANS), BF16),
            pltpu.VMEM((CHANS, HIDDEN), BF16),
            pltpu.VMEM((BASIS * GROUP, 2 * ORDERS * 128), BF16),
            pltpu.VMEM((ORDERS, 2 * GROUP, 128), F32),
            pltpu.VMEM((cells, CHANS), F32),
            pltpu.VMEM((cells, CHANS), BF16),
            pltpu.VMEM((cells, CHANS), BF16),
            pltpu.VMEM((BASIS, TAPS, TAPS, NLAT), BF16),
            pltpu.VMEM((TAPS, 2, NLAT), jnp.int32),
            pltpu.VMEM((2, GROUP, NLAT), F32),
            pltpu.VMEM((8, NLAT), F32),
            pltpu.SemaphoreType.DMA((12,)),
            pltpu.SemaphoreType.REGULAR,
            pltpu.SemaphoreType.DMA((10,)),
            pltpu.SemaphoreType.DMA((10,)),
        ],
        compiler_params=pltpu.CompilerParams(
            collective_id=0, has_side_effects=True, vmem_limit_bytes=60 * 1024 * 1024
        ),
        name="block",
    )(
        activations.reshape(cells, CHANS),
        cotangent.reshape(cells, CHANS),
        jnp.transpose(basis_weights, (0, 2, 3, 1)),
        jnp.transpose(extents, (2, 0, 1)),
        spec_filter,
        mix_weight,
        w_in,
        w_out,
        legendre_values(),
        trig_values(),
        phase_values(),
        quad_values(),
    )
    out, grad_x, grad_filter = (
        pltpu.with_memory_space_constraint(value, pltpu.VMEM) for value in (out, grad_x, grad_filter)
    )
    out, grad_x, grad_filter = pl.pallas_call(
        hand_out,
        out_shape=(
            jax.ShapeDtypeStruct((cells, CHANS), BF16),
            jax.ShapeDtypeStruct((cells, CHANS), BF16),
            jax.ShapeDtypeStruct((2 * GROUP, 128), F32),
        ),
        in_specs=[vmem] * 3,
        out_specs=(vmem,) * 3,
        name="hand_out",
    )(out, grad_x, grad_filter)
    return (
        out.reshape(ROWS, COLS, CHANS),
        grad_x.reshape(ROWS, COLS, CHANS),
        grad_filter.reshape(2, GROUP, 128),
    )


def solution(mesh):
    placed = (
        P("lat", "lon", None),
        P(),
        P(),
        P(),
        P(None, "lon", None),
        P(),
        P(),
        P("lat", "lon", None),
    )
    return jax.shard_map(
        local,
        mesh=mesh,
        in_specs=placed,
        out_specs=(P("lat", "lon", None), P("lat", "lon", None), P(None, "lon", None)),
        check_vma=False,
    )
```

```python
import math

import jax
import jax.numpy as jnp
import numpy as np
from jax import lax
from jax.experimental import pallas as pl
from jax.experimental.pallas import tpu as pltpu
from jax.sharding import PartitionSpec as P

EPSILON = 1e-05
MESH = pl.DeviceIdType.MESH
F32 = jnp.float32
BF16 = jnp.bfloat16

NLAT = 128
NLON = 512
CHANS = 256
HIDDEN = 512
BASIS = 9
GROUP = 16
TAPS = 7
REACH = 3
LATS = 32
ROWS = 4
COLS = 32
ORDERS = 4
PARTS = 8
NEAR = 8
FAR = 64
FIELD_STEPS = ((1, 16), (2, 64))
NEAREST = (4, 5, 3, 2, 6, 1, 7)
ORDER_STEPS = ((1, 16), (2, 32), (4, 64))
FARTHEST = (4, 3, 5, 2, 6, 1, 7, 0)


def legendre_values():
    theta = math.pi * (np.arange(NLAT) + 0.5) / NLAT
    cosine, sine = (np.cos(theta), np.sin(theta))
    table = np.zeros((NLAT, NLAT, NLAT))
    for order in range(NLAT):
        steps = np.arange(1, order + 1)
        growth = np.sum(0.5 * np.log((2.0 * steps + 1.0) / (2.0 * steps)))
        earlier = np.zeros(NLAT)
        latest = np.exp(-0.5 * math.log(4.0 * math.pi) + growth + order * np.log(sine))
        table[order, order] = latest
        for degree in range(order + 1, NLAT):
            upper = math.sqrt((4.0 * degree**2 - 1.0) / (degree**2 - order**2))
            below = degree - 1.0
            lower = math.sqrt((below**2 - order**2) / (4.0 * below**2 - 1.0))
            earlier, latest = (latest, upper * (cosine * latest - lower * earlier))
            table[order, degree] = latest
    return table.astype(np.float32).reshape(LATS, ORDERS, NLAT, NLAT)


def trig_values():
    table = np.zeros((2, ORDERS, 2, LATS, NEAR, COLS))
    order = 4 * np.arange(LATS)[None, :] + np.arange(ORDERS)[:, None]
    for half in range(2):
        for near in range(NEAR):
            lon = 32 * ((near // 2) * 4 + half * 2 + near % 2) + np.arange(COLS)
            angle = (order[:, :, None] * lon[None, None, :] % NLON) * (2.0 * math.pi / NLON)
            table[half, :, 0, :, near] = np.cos(angle)
            table[half, :, 1, :, near] = -np.sin(angle)
    return table.astype(np.float32).reshape(2, PARTS * LATS, NEAR * COLS)


def phase_values():
    order = 4 * np.arange(LATS)[:, None] + np.arange(ORDERS)[None, :]
    shift = np.arange(TAPS) - REACH
    angle = order[:, None, :] * shift[None, :, None] * (2.0 * math.pi / NLON)
    pairs = np.stack([np.cos(angle), np.sin(angle)], axis=-1).reshape(LATS, TAPS, PARTS, 1)
    return np.broadcast_to(pairs, (LATS, TAPS, PARTS, 128)).astype(np.float32).copy()


def quad_values():
    theta = math.pi * (np.arange(NLAT) + 0.5) / NLAT
    weights = (2.0 * math.pi / NLON) * (math.pi / NLAT) * np.sin(theta)
    return np.broadcast_to(weights[None], (8, NLAT)).astype(np.float32).copy()


def mm(left, right, left_dim=1, right_dim=0):
    return lax.dot_general(
        left, right, (((left_dim,), (right_dim,)), ((), ())), preferred_element_type=F32
    )


def swap_blocks(blocks, steps):
    blocks = list(blocks)
    lane = lax.broadcasted_iota(jnp.int32, blocks[0].shape, 1)
    for stride, width in steps:
        keep = (lane & width) == 0
        for at in range(len(blocks)):
            if at & stride == 0:
                low, high = (blocks[at], blocks[at | stride])
                blocks[at] = jnp.where(keep, low, pltpu.roll(high, width, 1))
                blocks[at | stride] = jnp.where(keep, pltpu.roll(low, 128 - width, 1), high)
    return blocks


def layer_norm(values):
    centred = values - jnp.mean(values, axis=1, keepdims=True)
    inverse = lax.rsqrt(jnp.mean(centred * centred, axis=1, keepdims=True) + EPSILON)
    return (centred * inverse, inverse)


def norm_back(normed, inverse, upstream):
    return inverse * (
        upstream
        - jnp.mean(upstream, axis=1, keepdims=True)
        - normed * jnp.mean(upstream * normed, axis=1, keepdims=True)
    )


def body(
    x_hbm,
    cot_hbm,
    basis_hbm,
    ext_hbm,
    filt_hbm,
    mix_hbm,
    win_hbm,
    wout_hbm,
    leg_hbm,
    trig_hbm,
    phase_hbm,
    quad_hbm,
    out_ref,
    gx_ref,
    gf_ref,
    send_near,
    recv_near,
    send_far,
    recv_far,
    grad_send,
    grad_recv,
    grad_row,
    grad_all,
    mix_v,
    win_v,
    wout_v,
    leg_v,
    leg_in,
    leg_out,
    trig_v,
    trig_down,
    trig_up,
    phase_v,
    taps_v,
    normed_v,
    dhid_v,
    wint_v,
    woutt_v,
    conv_v,
    coef_v,
    dcar_v,
    x_ref,
    cot_ref,
    basis_ref,
    ext_ref,
    filt_ref,
    quad_ref,
    load_sem,
    ring_sem,
    send_sem,
    recv_sem,
):
    lat = lax.axis_index("lat")
    lon = lax.axis_index("lon")
    x_at, half, core = (lon // 4, lax.rem(lon // 2, 2), lax.rem(lon, 2))
    near_me = x_at * 2 + core
    far_me = half * LATS + lat
    z_me, y_me = (far_me // 8, lax.rem(far_me, 8))

    def over_near(action):
        for move in NEAREST:
            peer = lax.rem(near_me + move, NEAR)
            action(peer, (lat, (peer // 2) * 4 + half * 2 + lax.rem(peer, 2)))

    def loop(count, action):
        def run(step, carry):
            action(step)
            return carry

        lax.fori_loop(0, count, run, 0)

    far_y = [lax.rem(y_me + move, 8) for move in FARTHEST]

    def far_device(peer_z, peer_y):
        peer_lat = lax.rem(peer_z, 4) * 8 + peer_y
        peer_lon = x_at * 4 + (peer_z // 4) * 2 + core
        return (peer_z * 8 + peer_y, peer_lat, (peer_lat, peer_lon))

    def over_far(action):
        def plane(step):
            away = (step + 1) // 2
            peer_z = lax.rem(z_me + 4 + away * (1 - 2 * lax.rem(step, 2)), 8)
            for peer_y in far_y:
                action(*far_device(peer_z, peer_y))

        loop(7, plane)
        for peer_y in far_y[:-1]:
            action(*far_device(z_me, peer_y))

    def ring_z(move):
        return far_device(lax.rem(z_me + move, 8), y_me)[2]

    barrier = pltpu.get_barrier_semaphore()

    def greet(device):
        pl.semaphore_signal(barrier, inc=1, device_id=device, device_id_type=MESH)

    over_near(lambda peer, device: greet(device))
    for move in FARTHEST[:-1]:
        greet(ring_z(move))
    for peer_y in far_y[:-1]:
        greet(far_device(z_me, peer_y)[2])

    loads = []
    for index, (source, target) in enumerate(
        (
            (x_hbm, x_ref),
            (ext_hbm, ext_ref),
            (basis_hbm, basis_ref),
            (trig_hbm.at[half], trig_v),
            (phase_hbm.at[lat], phase_v),
            (leg_hbm.at[lat], leg_v),
            (mix_hbm.at[:, lon], mix_v),
            (win_hbm, win_v),
            (wout_hbm, wout_v),
            (cot_hbm, cot_ref),
            (filt_hbm, filt_ref),
            (quad_hbm, quad_ref),
        )
    ):
        copy = pltpu.make_async_copy(source, target, load_sem.at[index])
        copy.start()
        loads.append(copy)

    def start_near(at):
        def action(peer, device):
            pltpu.make_async_remote_copy(
                src_ref=send_near.at[at, peer],
                dst_ref=recv_near.at[at, near_me],
                send_sem=send_sem.at[at],
                recv_sem=recv_sem.at[at],
                device_id=device,
                device_id_type=MESH,
            ).start()

        over_near(action)
        recv_near[at, near_me] = send_near[at, near_me]

    def wait_near(at):
        block = recv_near.at[at, pl.ds(0, NEAR - 1)]
        pltpu.make_async_copy(block, block, recv_sem.at[at]).wait()

    def start_far(at, both):
        def action(peer, peer_lat, device):
            pltpu.make_async_remote_copy(
                src_ref=send_far.at[at, peer_lat if both else peer],
                dst_ref=recv_far.at[at, far_me],
                send_sem=send_sem.at[4 + at],
                recv_sem=recv_sem.at[4 + at],
                device_id=device,
                device_id_type=MESH,
            ).start()

        over_far(action)
        recv_far[at, far_me] = send_far[at, lat if both else far_me]

    def wait_far(at):
        block = recv_far.at[at, pl.ds(0, FAR - 1)]
        pltpu.make_async_copy(block, block, recv_sem.at[4 + at]).wait()

    def fill_field(at, field):
        for side in range(2):
            blocks = swap_blocks(
                [
                    field[a * COLS : (a + 1) * COLS, side * 128 : (side + 1) * 128].astype(BF16)
                    for a in range(ROWS)
                ],
                FIELD_STEPS,
            )
            for near in range(4):
                send_near[at, side * 4 + near] = blocks[near]

    def take_field(at):
        sides = [
            jnp.concatenate(
                swap_blocks(
                    [recv_near[at, side * 4 + near] for near in range(4)], FIELD_STEPS
                ),
                axis=0,
            )
            for side in range(2)
        ]
        return jnp.concatenate(sides, axis=1).astype(F32)

    def spectrum_rows(flat, spot):
        row, part = (2 * (spot // 4) + spot % 2, spot // 2 % 2)
        return flat.at[pl.ds(part * LATS * ROWS + row, LATS, stride=ROWS), :]

    def to_spectrum(near_at, far_at):
        field = recv_near[near_at].reshape(NEAR * COLS, 128)
        parts = mm(trig_down[...], field)
        blocks = swap_blocks(
            [parts[at * LATS : (at + 1) * LATS] for at in range(PARTS)], ORDER_STEPS
        )
        flat = send_far.at[far_at].reshape(FAR * ROWS, 128)
        for spot in range(PARTS):
            spectrum_rows(flat, spot)[...] = blocks[spot]
        if far_at == 0:
            pl.semaphore_wait(ring_sem, 7)
        start_far(far_at, False)

    def take_spectrum(far_at):
        flat = recv_far.at[far_at].reshape(FAR * ROWS, 128)
        return (flat[0:NLAT, :] + flat[NLAT : 2 * NLAT, :]).T

    def send_spectrum(far_at, field):
        flat = send_far.at[far_at].reshape(FAR * ROWS, 128)
        flat[0:NLAT, :] = field.T
        start_far(far_at, True)

    def to_grid(far_at, near_at):
        flat = recv_far.at[far_at].reshape(FAR * ROWS, 128)
        rows = [spectrum_rows(flat, spot)[...].astype(BF16) for spot in range(PARTS)]
        stacked = jnp.concatenate(swap_blocks(rows, ORDER_STEPS), axis=0)
        field = mm(trig_up[...], stacked)
        send_near[near_at] = field.astype(BF16).reshape(NEAR, COLS, 128)
        start_near(near_at)

    def analyse(rows, at):
        return mm(rows.astype(BF16), leg_in[at])

    def synthesise(rows, at):
        return mm(rows.astype(BF16), leg_out[at])

    def order_weight(at):
        return jnp.where(lat * ORDERS + at == 0, 1.0, 2.0).astype(F32)

    loads[0].wait()
    normed, inverse_in = layer_norm(x_ref[...].astype(F32))
    normed_v[...] = normed
    fill_field(0, normed)
    pl.semaphore_wait(barrier, NEAR - 1 + 7 + 7)
    start_near(0)
    for move in FARTHEST[:-1]:
        pl.semaphore_signal(ring_sem, inc=1, device_id=ring_z(move), device_id_type=MESH)

    for copy in loads[1:5]:
        copy.wait()
    trig_down[...] = trig_v[...].astype(BF16)
    trig_up[...] = trig_v[...].T.astype(BF16)
    lat_at = lax.broadcasted_iota(jnp.int32, (TAPS, 128), 1)
    shift = lax.broadcasted_iota(jnp.int32, (TAPS, 128), 0) - REACH
    for r in range(TAPS):
        west, east = (ext_ref[r, 0:1, :], ext_ref[r, 1:2, :])
        inside = (shift >= -west) & (shift <= east)
        inside = inside & (lat_at + (r - REACH) >= 0) & (lat_at + (r - REACH) < NLAT)
        for k in range(BASIS):
            kept = jnp.where(inside, basis_ref[k, r].astype(F32), 0.0)
            total = phase_v[0] * kept[0:1]
            for d in range(1, TAPS):
                total = total + phase_v[d] * kept[d : d + 1]
            taps_v[k, r] = total
    for copy in loads[5:]:
        copy.wait()

    wait_near(0)
    to_spectrum(0, 0)

    for at in range(ORDERS):
        leg_out[at] = leg_v[at].astype(BF16)
        leg_in[at] = leg_v[at].T.astype(BF16)
    mix = mix_v[...].reshape(BASIS * GROUP, GROUP)
    wint_v[...] = win_v[...].T
    woutt_v[...] = wout_v[...].T
    dhid_v[...] = mm(cot_ref[...], woutt_v[...])
    quad = quad_ref[0:1, :]
    filter_real, filter_imag = (filt_ref[0], filt_ref[1])

    wait_far(0)
    spectrum = take_spectrum(0)
    for at in range(ORDERS):
        real = spectrum[at * 32 : at * 32 + 16]
        imag = spectrum[at * 32 + 16 : at * 32 + 32]
        sum_real = jnp.zeros((BASIS, GROUP, 128), F32)
        sum_imag = jnp.zeros((BASIS, GROUP, 128), F32)
        for r in range(TAPS):
            moved_real = pltpu.roll(real, (REACH - r) % 128, 1)[None]
            moved_imag = pltpu.roll(imag, (REACH - r) % 128, 1)[None]
            tap_real = taps_v[:, r, 2 * at : 2 * at + 1, :]
            tap_imag = taps_v[:, r, 2 * at + 1 : 2 * at + 2, :]
            sum_real = sum_real + (tap_real * moved_real - tap_imag * moved_imag)
            sum_imag = sum_imag + (tap_real * moved_imag + tap_imag * moved_real)
        conv_v[:, 2 * at * 128 : (2 * at + 1) * 128] = sum_real.reshape(144, 128).astype(BF16)
        conv_v[:, (2 * at + 1) * 128 : (2 * at + 2) * 128] = sum_imag.reshape(144, 128).astype(BF16)
    mixed = mm(mix, conv_v[...], 0, 0)
    pieces = []
    for at in range(ORDERS):
        rows = jnp.concatenate(
            [
                mixed[:, 2 * at * 128 : (2 * at + 1) * 128] * quad,
                mixed[:, (2 * at + 1) * 128 : (2 * at + 2) * 128] * quad,
            ],
            axis=0,
        )
        coefs = analyse(rows, at)
        coef_v[at] = coefs
        real, imag = (coefs[0:16], coefs[16:32])
        product = jnp.concatenate(
            [
                real * filter_real - imag * filter_imag,
                real * filter_imag + imag * filter_real,
            ],
            axis=0,
        )
        pieces.append(synthesise(product, at) * order_weight(at))
    send_spectrum(1, jnp.concatenate(pieces, axis=0))
    wait_far(1)
    to_grid(1, 1)
    wait_near(1)

    carried = x_ref[...].astype(F32) + take_field(1)
    normed_mid, inverse_mid = layer_norm(carried)
    preact = mm(normed_mid.astype(BF16), win_v[...])
    bell = jnp.exp(-0.5 * preact * preact) * (1.0 / math.sqrt(2.0 * math.pi))
    gate = 0.5 * (1.0 + lax.erf(preact * (1.0 / math.sqrt(2.0))))
    d_preact = (dhid_v[...] * (gate + preact * bell)).astype(BF16)
    d_normed = mm(d_preact, wint_v[...])
    d_carried = cot_ref[...].astype(F32) + norm_back(normed_mid, inverse_mid, d_normed)
    fill_field(2, d_carried)
    start_near(2)
    dcar_v[...] = d_carried
    hidden = (preact * gate).astype(BF16)
    out_ref[...] = (carried + mm(hidden, wout_v[...])).astype(BF16)

    wait_near(2)
    to_spectrum(2, 2)
    wait_far(2)
    spectrum = take_spectrum(2)
    grad_real = jnp.zeros((GROUP, 128), F32)
    grad_imag = jnp.zeros((GROUP, 128), F32)
    upstreams = []
    for at in range(ORDERS):
        upstream = analyse(spectrum[at * 32 : at * 32 + 32], at) * order_weight(at)
        up_real, up_imag = (upstream[0:16], upstream[16:32])
        upstreams.append((up_real, up_imag))
        real, imag = (coef_v[at, 0:16], coef_v[at, 16:32])
        grad_real = grad_real + (up_real * real + up_imag * imag)
        grad_imag = grad_imag + (up_imag * real - up_real * imag)

    flat = grad_send.reshape(2 * GROUP, 128)
    flat[0:GROUP, :] = grad_real
    flat[GROUP : 2 * GROUP, :] = grad_imag

    def column_peer(step):
        peer = lax.rem(lat + 1 + step, LATS)
        return (peer, (peer, lon))

    def scatter(step):
        peer, device = column_peer(step)
        pltpu.make_async_remote_copy(
            src_ref=grad_send.at[peer],
            dst_ref=grad_recv.at[lat],
            send_sem=send_sem.at[8],
            recv_sem=recv_sem.at[8],
            device_id=device,
            device_id_type=MESH,
        ).start()

    def gather(step):
        peer, device = column_peer(step)
        pltpu.make_async_remote_copy(
            src_ref=grad_row.at[0],
            dst_ref=grad_all.at[lat],
            send_sem=send_sem.at[9],
            recv_sem=recv_sem.at[9],
            device_id=device,
            device_id_type=MESH,
        ).start()

    for step in range(LATS - 1):
        scatter(step)
    grad_recv[lat] = grad_send[lat]

    pieces = []
    for at in range(ORDERS):
        up_real, up_imag = upstreams[at]
        d_coeff = jnp.concatenate(
            [
                up_real * filter_real + up_imag * filter_imag,
                up_imag * filter_real - up_real * filter_imag,
            ],
            axis=0,
        )
        rows = synthesise(d_coeff, at) * quad
        pieces.extend([rows[0:16], rows[16:32]])
    d_conv = mm(mix, jnp.concatenate(pieces, axis=1).astype(BF16))
    pieces = []
    for at in range(ORDERS):
        real = d_conv[:, 2 * at * 128 : (2 * at + 1) * 128].reshape(BASIS, GROUP, 128)
        imag = d_conv[:, (2 * at + 1) * 128 : (2 * at + 2) * 128].reshape(BASIS, GROUP, 128)
        sum_real = jnp.zeros((GROUP, 128), F32)
        sum_imag = jnp.zeros((GROUP, 128), F32)
        for r in range(TAPS):
            tap_real = taps_v[:, r, 2 * at : 2 * at + 1, :]
            tap_imag = taps_v[:, r, 2 * at + 1 : 2 * at + 2, :]
            row_real = jnp.sum(tap_real * real + tap_imag * imag, axis=0)
            row_imag = jnp.sum(tap_real * imag - tap_imag * real, axis=0)
            sum_real = sum_real + pltpu.roll(row_real, (r - REACH) % 128, 1)
            sum_imag = sum_imag + pltpu.roll(row_imag, (r - REACH) % 128, 1)
        pieces.extend([sum_real, sum_imag])
    send_spectrum(3, jnp.concatenate(pieces, axis=0))

    block = grad_recv.at[pl.ds(0, LATS - 1)]
    pltpu.make_async_copy(block, block, recv_sem.at[8]).wait()
    grad_row[0] = jnp.sum(grad_recv[...], axis=0)
    loop(LATS - 1, gather)
    grad_all[lat] = grad_row[0]

    wait_far(3)
    to_grid(3, 3)

    wait_near(3)
    d_normed_in = take_field(3)
    grad_x = dcar_v[...] + norm_back(normed_v[...], inverse_in, d_normed_in)
    gx_ref[...] = grad_x.astype(BF16)

    block = grad_all.at[pl.ds(0, LATS - 1)]
    pltpu.make_async_copy(block, block, recv_sem.at[9]).wait()
    gf_ref[...] = grad_all.reshape(2 * GROUP, 128)[...]

    for at in range(4):
        block = send_near.at[at, pl.ds(0, NEAR - 1)]
        pltpu.make_async_copy(block, block, send_sem.at[at]).wait()
        block = send_far.at[at, pl.ds(0, FAR - 1)]
        pltpu.make_async_copy(block, block, send_sem.at[4 + at]).wait()
    block = grad_send.at[pl.ds(0, LATS - 1)]
    pltpu.make_async_copy(block, block, send_sem.at[8]).wait()
    pltpu.make_async_copy(block, block, send_sem.at[9]).wait()


def hand_out(first, second, third, first_out, second_out, third_out):
    first_out[...] = first[...]
    second_out[...] = second[...]
    third_out[...] = third[...]


def local(activations, basis_weights, extents, mix_weight, spec_filter, w_in, w_out, cotangent):
    cells = ROWS * COLS
    vmem = pl.BlockSpec(memory_space=pltpu.VMEM)
    hbm = pl.BlockSpec(memory_space=pltpu.HBM)
    out, grad_x, grad_filter = pl.pallas_call(
        body,
        out_shape=(
            pltpu.VMEM((cells, CHANS), BF16),
            pltpu.VMEM((cells, CHANS), BF16),
            pltpu.VMEM((2 * GROUP, 128), F32),
        ),
        in_specs=[hbm] * 12,
        out_specs=(vmem, vmem, vmem),
        scratch_shapes=[
            pltpu.VMEM((4, NEAR, 2 * GROUP, 128), BF16),
            pltpu.VMEM((4, NEAR, 2 * GROUP, 128), BF16),
            pltpu.VMEM((4, FAR, ROWS, 128), F32),
            pltpu.VMEM((4, FAR, ROWS, 128), F32),
            pltpu.VMEM((LATS, 1, 128), F32),
            pltpu.VMEM((LATS, 1, 128), F32),
            pltpu.VMEM((1, 1, 128), F32),
            pltpu.VMEM((LATS, 1, 128), F32),
            pltpu.VMEM((BASIS, GROUP, GROUP), BF16),
            pltpu.VMEM((CHANS, HIDDEN), BF16),
            pltpu.VMEM((HIDDEN, CHANS), BF16),
            pltpu.VMEM((ORDERS, NLAT, NLAT), F32),
            pltpu.VMEM((ORDERS, NLAT, NLAT), BF16),
            pltpu.VMEM((ORDERS, NLAT, NLAT), BF16),
            pltpu.VMEM((PARTS * LATS, NEAR * COLS), F32),
            pltpu.VMEM((PARTS * LATS, NEAR * COLS), BF16),
            pltpu.VMEM((NEAR * COLS, PARTS * LATS), BF16),
            pltpu.VMEM((TAPS, PARTS, 128), F32),
            pltpu.VMEM((BASIS, TAPS, PARTS, 128), F32),
            pltpu.VMEM((cells, CHANS), F32),
            pltpu.VMEM((cells, HIDDEN), F32),
            pltpu.VMEM((HIDDEN, CHANS), BF16),
            pltpu.VMEM((CHANS, HIDDEN), BF16),
            pltpu.VMEM((BASIS * GROUP, 2 * ORDERS * 128), BF16),
            pltpu.VMEM((ORDERS, 2 * GROUP, 128), F32),
            pltpu.VMEM((cells, CHANS), F32),
            pltpu.VMEM((cells, CHANS), BF16),
            pltpu.VMEM((cells, CHANS), BF16),
            pltpu.VMEM((BASIS, TAPS, TAPS, NLAT), BF16),
            pltpu.VMEM((TAPS, 2, NLAT), jnp.int32),
            pltpu.VMEM((2, GROUP, NLAT), F32),
            pltpu.VMEM((8, NLAT), F32),
            pltpu.SemaphoreType.DMA((12,)),
            pltpu.SemaphoreType.REGULAR,
            pltpu.SemaphoreType.DMA((10,)),
            pltpu.SemaphoreType.DMA((10,)),
        ],
        compiler_params=pltpu.CompilerParams(
            collective_id=0, has_side_effects=True, vmem_limit_bytes=60 * 1024 * 1024
        ),
        name="block",
    )(
        activations.reshape(cells, CHANS),
        cotangent.reshape(cells, CHANS),
        jnp.transpose(basis_weights, (0, 2, 3, 1)),
        jnp.transpose(extents, (2, 0, 1)),
        spec_filter,
        mix_weight,
        w_in,
        w_out,
        legendre_values(),
        trig_values(),
        phase_values(),
        quad_values(),
    )
    out, grad_x, grad_filter = (
        pltpu.with_memory_space_constraint(value, pltpu.VMEM) for value in (out, grad_x, grad_filter)
    )
    out, grad_x, grad_filter = pl.pallas_call(
        hand_out,
        out_shape=(
            jax.ShapeDtypeStruct((cells, CHANS), BF16),
            jax.ShapeDtypeStruct((cells, CHANS), BF16),
            jax.ShapeDtypeStruct((2 * GROUP, 128), F32),
        ),
        in_specs=[vmem] * 3,
        out_specs=(vmem,) * 3,
        name="hand_out",
    )(out, grad_x, grad_filter)
    return (
        out.reshape(ROWS, COLS, CHANS),
        grad_x.reshape(ROWS, COLS, CHANS),
        grad_filter.reshape(2, GROUP, 128),
    )


def solution(mesh):
    placed = (
        P("lat", "lon", None),
        P(),
        P(),
        P(),
        P(None, "lon", None),
        P(),
        P(),
        P("lat", "lon", None),
    )
    return jax.shard_map(
        local,
        mesh=mesh,
        in_specs=placed,
        out_specs=(P("lat", "lon", None), P("lat", "lon", None), P(None, "lon", None)),
        check_vma=False,
    )
```
